32 devices in a mesh: grp: 2 (over y), row: 4 (over x, core), col: 4 (over z).
Axes of the slice: x: 2, y: 2, z: 4, core: 2. Of those that a mesh axis runs over, the one named last changes fastest.
Arguments:
- object_field: float32 [4, 2, 1024, 1024], P('grp', None, 'row', 'col'), parts along dimension 0, may hold values from -4.2 to 4.2
- probe_modes: float32 [6, 2, 256, 256], P('grp'), parts along dimension 0, may hold values from -2.4 to 2.4
- measured: float32 [8, 4, 2, 256, 256], P(('grp', 'row'), 'col'), parts along dimension 0, may hold values from 0.2 to 3
- offsets: int32 [8, 4, 2, 2], P(('grp', 'row'), 'col'), parts along dimension 0, may hold values from -64 to 64, as said below
Outputs:
- object_grad: float32 [4, 2, 1024, 1024], P('grp', None, 'row', 'col'), parts along dimension 0
- new_probe: float32 [6, 2, 256, 256], P('grp'), parts along dimension 0
The draws below stay inside these ranges and needn't reach their ends.
There are 2 independent parts, one for each index of `grp`. The reference program is written for one: setup_inputs(seed, part) draws one part's arguments, and reference() takes and returns one part's arrays. A program takes and returns all parts, laid end to end along the dimension named above; each array names one. Nothing has to cross between parts.
Inputs may be any that keep to these rules, and one draw needn't show every extreme that they name: Windows of the first and last tile rows and columns stay inside the object; a tile's row offsets reach at most 64 and its column offsets at most 64.
All inputs are finite; a program needn't handle non-finite values.
Results may differ from the reference program's by a relative error of at most 0.00013.
Values sent between devices are 32-bit elements; how exact they have to be, the bound alone decides.
A program may use at most 128 MiB of HBM per device.

```python
import math
import jax
import jax.numpy as jnp
from jax import lax

NP = 256
MODES = 3
SLICES = 2
HALO = 64
CH = 256
CW = 256
POS_DEV = 2
NY = 1024
NX = 1024
N_ROW = 4
N_COL = 4


def draw_offsets(key, part):
    key = jax.random.fold_in(key, 11)
    key_rows, key_cols, key_pick_row, key_pick_col = jax.random.split(key, 4)
    grid_shape = (N_ROW, N_COL, POS_DEV)
    lowest = -HALO
    high_rows = CH + HALO - NP
    high_cols = CW + HALO - NP
    rows_off = jax.random.randint(key_rows, grid_shape, lowest, high_rows + 1)
    cols_off = jax.random.randint(key_cols, grid_shape, lowest, high_cols + 1)
    tile_r = jnp.broadcast_to(jnp.arange(N_ROW)[:, None, None], grid_shape)
    tile_c = jnp.broadcast_to(jnp.arange(N_COL)[None, :, None], grid_shape)
    position = jnp.broadcast_to(jnp.arange(POS_DEV)[None, None, :], grid_shape)
    pick_row = jax.random.randint(key_pick_row, (), 1, N_ROW - 1)
    pick_col = jax.random.randint(key_pick_col, (), 1, N_COL - 1)
    other_col = 1 + pick_col % (N_COL - 2)
    first_tile = (tile_r == pick_row) & (tile_c == pick_col) & (position == 0)
    second_tile = (tile_r == pick_row) & (tile_c == other_col) & (position == 0)
    rows_off = jnp.where(first_tile, lowest, jnp.where(second_tile, high_rows, rows_off))
    cols_off = jnp.where(first_tile, high_cols, jnp.where(second_tile, lowest, cols_off))
    rows_off = jnp.where(tile_r == 0, jnp.maximum(rows_off, 0), rows_off)
    rows_off = jnp.where(tile_r == N_ROW - 1, jnp.minimum(rows_off, CH - NP), rows_off)
    cols_off = jnp.where(tile_c == 0, jnp.maximum(cols_off, 0), cols_off)
    cols_off = jnp.where(tile_c == N_COL - 1, jnp.minimum(cols_off, CW - NP), cols_off)
    return jnp.stack([rows_off, cols_off], axis=-1).astype(jnp.int32)


def levels(own_key, shape, shards, least, top_value):
    def one(axis_at, shards_of):
        steps = jax.random.uniform(jax.random.fold_in(jax.random.fold_in(own_key, 6), axis_at), (shards_of,), jnp.float32, least / len(shards), top_value / len(shards))
        return jnp.repeat(jnp.exp(steps), shape[axis_at] // shards_of).reshape((-1,) + (1,) * (len(shape) - axis_at - 1))

    level = one(*shards[0])
    for cut in shards[1:]:
        level = level * one(*cut)
    return level


def gaussian(rng, shape, scale, bound, cuts=(), kind=jnp.bfloat16):
    values = scale * jax.random.normal(rng, shape, jnp.float32)
    if cuts:
        values = values * levels(rng, shape, cuts, -0.22, 0.18)
    return jnp.clip(values, -bound, bound).astype(kind)


def setup_inputs(seed: int = 0, part: int = 0) -> dict:
    arg_keys = jax.random.split(jax.random.key(seed), 5)
    part_splits = jax.random.split(jax.random.fold_in(arg_keys[4], part), 5)
    return {
        "object_field": gaussian(part_splits[0], (SLICES, 2, NY, NX), 0.7, 4.2, ((2, 4), (3, 4)), jnp.float32),
        "probe_modes": gaussian(part_splits[1], (MODES, 2, NP, NP), 0.4, 2.4, (), jnp.float32),
        "measured": jnp.clip(jnp.exp(math.log(3.0) - 2.7080502 * jax.random.uniform(part_splits[2], (N_ROW, N_COL, POS_DEV, NP, NP), jnp.float32) ** levels(part_splits[2], (N_ROW, N_COL, POS_DEV, NP, NP), ((0, 4), (1, 4)), -0.2, 0.2)), 0.2, 3.0),
        "offsets": draw_offsets(jax.random.fold_in(jax.random.fold_in(arg_keys[4], part), 71), part),
    }


EPSILON = 1e-06
PROP_PHASE = 40.0

def propagator():
    indices = jnp.arange(NP, dtype=jnp.int32)
    frequency = ((indices + NP // 2) % NP - NP // 2).astype(jnp.float32) / NP
    radius_sq = frequency[:, None] ** 2 + frequency[None, :] ** 2
    return lax.complex(jnp.cos(PROP_PHASE * radius_sq), -jnp.sin(PROP_PHASE * radius_sq))

def forward_two(field_in):
    return jnp.fft.fft2(field_in, norm='ortho')

def inverse_two(field_in):
    return jnp.fft.ifft2(field_in, norm='ortho')

def position_gradient(window, mode_waves, pattern, kernel):
    entering = []
    wave_field = mode_waves
    far_field = mode_waves
    for slice_index in range(SLICES):
        entering.append(wave_field)
        exit_wave = window[slice_index][None] * wave_field
        if slice_index < SLICES - 1:
            wave_field = inverse_two(kernel * forward_two(exit_wave))
        else:
            far_field = forward_two(exit_wave)
    intensity = lax.optimization_barrier(jnp.sum(jnp.real(far_field) ** 2 + jnp.imag(far_field) ** 2, axis=0))
    misfit = intensity - pattern
    backward = inverse_two(misfit[None] * far_field)
    gradients = [None] * SLICES
    before_layer = backward
    for slice_index in range(SLICES - 1, -1, -1):
        gradients[slice_index] = lax.optimization_barrier(jnp.sum(jnp.conj(entering[slice_index]) * backward, axis=0))
        before_layer = jnp.conj(window[slice_index])[None] * backward
        if slice_index > 0:
            backward = inverse_two(jnp.conj(kernel) * forward_two(before_layer))
    return (jnp.stack(gradients), before_layer)

def orthogonalize(updated):
    basis = []
    for mode_index in range(MODES):
        vector = updated[mode_index]
        for earlier in basis:
            inner_prod = jnp.sum(jnp.conj(earlier) * updated[mode_index])
            norm_sq = jnp.sum(jnp.real(earlier) ** 2 + jnp.imag(earlier) ** 2)
            vector = vector - inner_prod / (norm_sq + EPSILON) * earlier
        basis.append(vector)
    return jnp.stack(basis)

def reference(object_field, probe_modes, measured, offsets):
    object_wave = lax.complex(object_field[:, 0], object_field[:, 1])
    padded = jnp.pad(object_wave, ((0, 0), (HALO, HALO), (HALO, HALO)))
    mode_waves = lax.complex(probe_modes[:, 0], probe_modes[:, 1])
    kernel = propagator()
    position_count = N_ROW * N_COL * POS_DEV
    flat_offsets = offsets.reshape(position_count, 2).astype(jnp.int32)
    counter = jnp.arange(position_count, dtype=jnp.int32)
    tile_row = counter // (N_COL * POS_DEV)
    tile_col = counter // POS_DEV % N_COL
    start_row = (tile_row * CH + flat_offsets[:, 0] + HALO).astype(jnp.int32)
    start_col = (tile_col * CW + flat_offsets[:, 1] + HALO).astype(jnp.int32)
    patterns = measured.reshape(position_count, NP, NP)
    zero_index = jnp.zeros((), jnp.int32)

    def accumulate(running, position):
        grad_padded, grad_probe = running
        row_start, col_start, pattern = position
        anchor = (zero_index, row_start, col_start)
        window = lax.dynamic_slice(padded, anchor, (SLICES, NP, NP))
        gradients, probe_term = position_gradient(window, mode_waves, pattern, kernel)
        current = lax.dynamic_slice(grad_padded, anchor, (SLICES, NP, NP))
        grad_padded = lax.dynamic_update_slice(grad_padded, current + gradients, anchor)
        return ((grad_padded, grad_probe + probe_term), None)
    initial = (jnp.zeros_like(padded), jnp.zeros_like(mode_waves))
    (grad_padded, grad_probe), unused = lax.scan(accumulate, initial, (start_row, start_col, patterns))
    inner_grad = grad_padded[:, HALO:HALO + NY, HALO:HALO + NX]
    object_grad = jnp.stack([jnp.real(inner_grad), jnp.imag(inner_grad)], axis=1)
    probe_sq = jnp.sum(probe_modes * probe_modes)
    grad_sq = jnp.sum(jnp.real(grad_probe) ** 2 + jnp.imag(grad_probe) ** 2) + EPSILON
    factor = 0.5 * jnp.sqrt(probe_sq / grad_sq)
    updated = mode_waves - factor * grad_probe
    modes_out = orthogonalize(updated)
    new_probe = jnp.stack([jnp.real(modes_out), jnp.imag(modes_out)], axis=1)
    return (object_grad, new_probe)
```

```python
import functools
import math

import jax
import jax.numpy as jnp
import numpy as np
from jax import lax
from jax.experimental import pallas as pl
from jax.experimental.pallas import tpu as pltpu
from jax.sharding import PartitionSpec as P

HALO = 64
EPSILON = 1e-06
PROP_PHASE = 40.0


def shifted(block, axis, distance):
    devices = range(lax.axis_size(axis))
    route = [(i - distance, i) for i in devices if i - distance in devices]
    return lax.ppermute(block, axis, route)


def with_halo(block, sides, width):
    for axis, dim in sides:
        count = lax.axis_size(axis)
        forward = [(i, i + 1) for i in range(count - 1)]
        backward = [(target, source) for source, target in forward]
        low = lax.ppermute(
            lax.slice_in_dim(block, block.shape[dim] - width, None, axis=dim), axis, forward
        )
        high = lax.ppermute(lax.slice_in_dim(block, 0, width, axis=dim), axis, backward)
        block = jnp.concatenate([low, block, high], axis=dim)
    return block


def split_tables(size):
    index = np.arange(size)
    turn = (index[:, None] * index[None, :]) % size
    dft = np.exp(-2j * np.pi * turn / size) / math.sqrt(size)
    freq = ((index + size // 2) % size - size // 2) / size
    prop = np.conj(dft) @ (np.exp(-1j * PROP_PHASE * freq**2)[:, None] * dft)
    stacked = []
    for matrix in (dft, prop):
        for part in (matrix.real, matrix.imag - matrix.real, matrix.imag + matrix.real):
            high = part.astype(jnp.bfloat16)
            low = (part - high.astype(np.float64)).astype(jnp.bfloat16)
            stacked.append(np.stack([high, low]))
    return np.stack(stacked)


def split(value):
    high = value.astype(jnp.bfloat16)
    return high, (value - high.astype(jnp.float32)).astype(jnp.bfloat16)


def mul_right(value, tab, k):
    high, low = split(value)
    t_high, t_low = tab[k, 0], tab[k, 1]
    return jnp.dot(
        jnp.concatenate([high, low, high], axis=1),
        jnp.concatenate([t_high, t_high, t_low], axis=0),
        preferred_element_type=jnp.float32,
    )


def mul_left(value, tab, k):
    high, low = split(value)
    t_high, t_low = tab[k, 0], tab[k, 1]
    return jnp.dot(
        jnp.concatenate([t_high, t_high, t_low], axis=1),
        jnp.concatenate([high, low, high], axis=0),
        preferred_element_type=jnp.float32,
    )


def both_sides(re, im, tab, base, conj):
    for mul in (mul_right, mul_left):
        both = mul(re + im, tab, base)
        if conj:
            re, im = both + mul(im, tab, base + 1), both - mul(re, tab, base + 2)
        else:
            re, im = both - mul(im, tab, base + 2), both + mul(re, tab, base + 1)
    return re, im


def gradient_kernel(offs, ext, probe, meas, tab, grad, pgrad, win, wave, far, inten, terms):
    modes, size = probe.shape[0], probe.shape[2]
    layers, wide = ext.shape[0], ext.shape[3]
    positions = meas.shape[2]
    grad[...] = jnp.zeros_like(grad)
    pgrad[...] = jnp.zeros_like(pgrad)

    def position(p, carry):
        row = offs[0, 0, p, 0] + HALO
        col = offs[0, 0, p, 1] + HALO
        base = pl.multiple_of(jnp.minimum(row // 8, (2 * HALO - 8) // 8) * 8, 8)
        rest = row - base
        tall = size + 8
        for l in range(layers):
            for c in range(2):
                rows = ext[l, c, pl.ds(base, tall), :]
                rows = pltpu.roll(rows, lax.rem(wide - col, wide), 1)[:, :size]
                win[l, c] = pltpu.roll(rows, lax.rem(tall - rest, tall), 0)[:size]
        inten[...] = -meas[0, 0, p]
        terms[...] = jnp.zeros_like(terms)
        last = layers - 1

        def forward(m, carry):
            re, im = probe[m, 0], probe[m, 1]
            for l in range(layers):
                t_re, t_im = win[l, 0], win[l, 1]
                e_re = t_re * re - t_im * im
                e_im = t_re * im + t_im * re
                if l < last:
                    re, im = both_sides(e_re, e_im, tab, 3, False)
                    wave[l, m, 0] = re
                    wave[l, m, 1] = im
                else:
                    re, im = both_sides(e_re, e_im, tab, 0, False)
            far[m, 0] = re
            far[m, 1] = im
            inten[...] += re * re + im * im
            return carry

        lax.fori_loop(0, modes, forward, 0, unroll=UNROLL)

        def backward(m, carry):
            misfit = inten[...]
            re, im = both_sides(misfit * far[m, 0], misfit * far[m, 1], tab, 0, True)
            for l in range(last, -1, -1):
                w_re = wave[l - 1, m, 0] if l > 0 else probe[m, 0]
                w_im = wave[l - 1, m, 1] if l > 0 else probe[m, 1]
                terms[l, 0] += w_re * re + w_im * im
                terms[l, 1] += w_re * im - w_im * re
                t_re, t_im = win[l, 0], win[l, 1]
                b_re = t_re * re + t_im * im
                b_im = t_re * im - t_im * re
                if l > 0:
                    re, im = both_sides(b_re, b_im, tab, 3, True)
                else:
                    pgrad[m, 0] += b_re
                    pgrad[m, 1] += b_im
            return carry

        lax.fori_loop(0, modes, backward, 0, unroll=UNROLL)
        for l in range(layers):
            for c in range(2):
                padded = jnp.concatenate([terms[l, c], jnp.zeros((8, size), jnp.float32)], axis=0)
                padded = pltpu.roll(padded, rest, 0)
                padded = jnp.concatenate(
                    [padded, jnp.zeros((tall, wide - size), jnp.float32)], axis=1
                )
                grad[l, c, pl.ds(base, tall), :] += pltpu.roll(padded, col, 1)
        return carry

    lax.fori_loop(0, positions, position, 0)


UNROLL = True


def total(value):
    return jnp.sum(jnp.sum(value, axis=0, keepdims=True), axis=1, keepdims=True)


def update_modes(probe, summed, out):
    modes = probe.shape[0]
    probe_sq = total(sum(probe[m, c] * probe[m, c] for m in range(modes) for c in range(2)))
    grad_sq = total(sum(summed[m, c] * summed[m, c] for m in range(modes) for c in range(2)))
    factor = 0.5 * jnp.sqrt(probe_sq / (grad_sq + EPSILON))
    norms = []
    for k in range(modes):
        out[k, 0] = probe[k, 0] - factor * summed[k, 0]
        out[k, 1] = probe[k, 1] - factor * summed[k, 1]
        ratios = []
        for a in range(k):
            inner_re = total(out[a, 0] * out[k, 0] + out[a, 1] * out[k, 1])
            inner_im = total(out[a, 0] * out[k, 1] - out[a, 1] * out[k, 0])
            ratios.append((inner_re / norms[a], inner_im / norms[a]))
        if k:
            re, im = out[k, 0], out[k, 1]
            for a, (r_re, r_im) in enumerate(ratios):
                re = re - (r_re * out[a, 0] - r_im * out[a, 1])
                im = im - (r_re * out[a, 1] + r_im * out[a, 0])
            out[k, 0] = re
            out[k, 1] = im
        norms.append(total(out[k, 0] * out[k, 0] + out[k, 1] * out[k, 1]) + EPSILON)


def gradients(offsets, extended, probe_modes, measured):
    modes, _, size, _ = probe_modes.shape
    layers = extended.shape[0]
    vmem = pl.BlockSpec(memory_space=pltpu.VMEM)
    f32 = jnp.float32
    tables = jnp.asarray(split_tables(size))
    return pl.pallas_call(
        gradient_kernel,
        out_shape=(
            jax.ShapeDtypeStruct(extended.shape, f32),
            jax.ShapeDtypeStruct(probe_modes.shape, f32),
        ),
        in_specs=[pl.BlockSpec(memory_space=pltpu.SMEM), vmem, vmem, vmem, vmem],
        out_specs=(vmem, vmem),
        scratch_shapes=[
            pltpu.VMEM((layers, 2, size, size), f32),
            pltpu.VMEM((max(layers - 1, 1), modes, 2, size, size), f32),
            pltpu.VMEM((modes, 2, size, size), f32),
            pltpu.VMEM((size, size), f32),
            pltpu.VMEM((layers, 2, size, size), f32),
        ],
        compiler_params=pltpu.CompilerParams(vmem_limit_bytes=48 << 20),
    )(offsets, extended, probe_modes, measured, tables)


def new_modes(probe_modes, summed):
    return pl.pallas_call(
        update_modes,
        out_shape=jax.ShapeDtypeStruct(probe_modes.shape, jnp.float32),
        compiler_params=pltpu.CompilerParams(vmem_limit_bytes=32 << 20),
    )(probe_modes, summed)


def fold(edge_grad, axis, dim):
    count = edge_grad.shape[dim]
    cut = functools.partial(lax.slice_in_dim, edge_grad, axis=dim)
    from_high = shifted(cut(0, HALO), axis, -1)
    from_low = shifted(cut(count - HALO, count), axis, 1)
    return jnp.concatenate(
        [
            cut(HALO, 2 * HALO) + from_low,
            cut(2 * HALO, count - 2 * HALO),
            cut(count - 2 * HALO, count - HALO) + from_high,
        ],
        axis=dim,
    )


def shards(object_field, probe_modes, measured, offsets):
    extended = with_halo(object_field, (("row", 2), ("col", 3)), HALO)
    grad_ext, local_grad = gradients(offsets, extended, probe_modes, measured)
    summed = lax.psum(local_grad, ("row", "col"))
    object_grad = fold(fold(grad_ext, "row", 2), "col", 3)
    return (object_grad, new_modes(probe_modes, summed))


def solution(mesh):
    placed = (
        P("grp", None, "row", "col"),
        P("grp", None, None, None),
        P(("grp", "row"), "col", None, None, None),
        P(("grp", "row"), "col", None, None),
    )
    return jax.shard_map(
        shards,
        mesh=mesh,
        in_specs=placed,
        out_specs=(P("grp", None, "row", "col"), P("grp", None, None, None)),
        check_vma=False,
    )
```

```python
import functools
import math

import jax
import jax.numpy as jnp
import numpy as np
from jax import lax
from jax.experimental import pallas as pl
from jax.experimental.pallas import tpu as pltpu
from jax.sharding import PartitionSpec as P

HALO = 64
EPSILON = 1e-06
PROP_PHASE = 40.0


def with_halo(block, sides, width):
    for axis, dim in sides:
        count = lax.axis_size(axis)
        forward = [(i, i + 1) for i in range(count - 1)]
        backward = [(target, source) for source, target in forward]
        low = lax.ppermute(
            lax.slice_in_dim(block, block.shape[dim] - width, None, axis=dim), axis, forward
        )
        high = lax.ppermute(lax.slice_in_dim(block, 0, width, axis=dim), axis, backward)
        block = jnp.concatenate([low, block, high], axis=dim)
    return block


def split_tables(size):
    index = np.arange(size)
    turn = (index[:, None] * index[None, :]) % size
    dft = np.exp(-2j * np.pi * turn / size) / math.sqrt(size)
    freq = ((index + size // 2) % size - size // 2) / size
    prop = np.conj(dft) @ (np.exp(-1j * PROP_PHASE * freq**2)[:, None] * dft)
    stacked = []
    for matrix in (dft, prop):
        for part in (matrix.real, matrix.imag - matrix.real, matrix.imag + matrix.real):
            high = part.astype(jnp.bfloat16)
            low = (part - high.astype(np.float64)).astype(jnp.bfloat16)
            stacked.append(np.stack([high, low]))
    return np.stack(stacked)


def split(value):
    high = value.astype(jnp.bfloat16)
    return high, (value - high.astype(jnp.float32)).astype(jnp.bfloat16)


def mul_right(value, tab, k):
    high, low = split(value)
    t_high, t_low = tab[k, 0], tab[k, 1]
    return jnp.dot(
        jnp.concatenate([high, low, high], axis=1),
        jnp.concatenate([t_high, t_high, t_low], axis=0),
        preferred_element_type=jnp.float32,
    )


def mul_left(value, tab, k):
    high, low = split(value)
    t_high, t_low = tab[k, 0], tab[k, 1]
    return jnp.dot(
        jnp.concatenate([t_high, t_high, t_low], axis=1),
        jnp.concatenate([high, low, high], axis=0),
        preferred_element_type=jnp.float32,
    )


def both_sides(re, im, tab, base, conj):
    for mul in (mul_right, mul_left):
        both = mul(re + im, tab, base)
        if conj:
            re, im = both + mul(im, tab, base + 1), both - mul(re, tab, base + 2)
        else:
            re, im = both - mul(im, tab, base + 2), both + mul(re, tab, base + 1)
    return re, im


def gradient_kernel(offs, ext, probe, meas, tab, grad, pgrad, win, wave, far, inten, terms):
    modes, size = probe.shape[0], probe.shape[2]
    layers, wide = ext.shape[0], ext.shape[3]
    positions = meas.shape[2]
    grad[...] = jnp.zeros_like(grad)
    pgrad[...] = jnp.zeros_like(pgrad)

    def position(p, carry):
        row = offs[0, 0, p, 0] + HALO
        col = offs[0, 0, p, 1] + HALO
        base = pl.multiple_of(jnp.minimum(row // 8, (2 * HALO - 8) // 8) * 8, 8)
        rest = row - base
        tall = size + 8
        for l in range(layers):
            for c in range(2):
                rows = ext[l, c, pl.ds(base, tall), :]
                rows = pltpu.roll(rows, lax.rem(wide - col, wide), 1)[:, :size]
                win[l, c] = pltpu.roll(rows, lax.rem(tall - rest, tall), 0)[:size]
        inten[...] = -meas[0, 0, p]
        terms[...] = jnp.zeros_like(terms)
        last = layers - 1

        def forward(m, carry):
            re, im = probe[m, 0], probe[m, 1]
            for l in range(layers):
                t_re, t_im = win[l, 0], win[l, 1]
                e_re = t_re * re - t_im * im
                e_im = t_re * im + t_im * re
                if l < last:
                    re, im = both_sides(e_re, e_im, tab, 3, False)
                    wave[l, m, 0] = re
                    wave[l, m, 1] = im
                else:
                    re, im = both_sides(e_re, e_im, tab, 0, False)
            far[m, 0] = re
            far[m, 1] = im
            inten[...] += re * re + im * im
            return carry

        lax.fori_loop(0, modes, forward, 0, unroll=UNROLL)

        def backward(m, carry):
            misfit = inten[...]
            re, im = both_sides(misfit * far[m, 0], misfit * far[m, 1], tab, 0, True)
            for l in range(last, -1, -1):
                w_re = wave[l - 1, m, 0] if l > 0 else probe[m, 0]
                w_im = wave[l - 1, m, 1] if l > 0 else probe[m, 1]
                terms[l, 0] += w_re * re + w_im * im
                terms[l, 1] += w_re * im - w_im * re
                t_re, t_im = win[l, 0], win[l, 1]
                b_re = t_re * re + t_im * im
                b_im = t_re * im - t_im * re
                if l > 0:
                    re, im = both_sides(b_re, b_im, tab, 3, True)
                else:
                    pgrad[m, 0] += b_re
                    pgrad[m, 1] += b_im
            return carry

        lax.fori_loop(0, modes, backward, 0, unroll=UNROLL)
        for l in range(layers):
            for c in range(2):
                padded = jnp.concatenate([terms[l, c], jnp.zeros((8, size), jnp.float32)], axis=0)
                padded = pltpu.roll(padded, rest, 0)
                padded = jnp.concatenate(
                    [padded, jnp.zeros((tall, wide - size), jnp.float32)], axis=1
                )
                grad[l, c, pl.ds(base, tall), :] += pltpu.roll(padded, col, 1)
        return carry

    lax.fori_loop(0, positions, position, 0)


UNROLL = True


def total(value):
    return jnp.sum(jnp.sum(value, axis=0, keepdims=True), axis=1, keepdims=True)


def update_modes(probe, summed, out):
    modes = probe.shape[0]
    probe_sq = total(sum(probe[m, c] * probe[m, c] for m in range(modes) for c in range(2)))
    grad_sq = total(sum(summed[m, c] * summed[m, c] for m in range(modes) for c in range(2)))
    factor = 0.5 * jnp.sqrt(probe_sq / (grad_sq + EPSILON))
    norms = []
    for k in range(modes):
        out[k, 0] = probe[k, 0] - factor * summed[k, 0]
        out[k, 1] = probe[k, 1] - factor * summed[k, 1]
        ratios = []
        for a in range(k):
            inner_re = total(out[a, 0] * out[k, 0] + out[a, 1] * out[k, 1])
            inner_im = total(out[a, 0] * out[k, 1] - out[a, 1] * out[k, 0])
            ratios.append((inner_re / norms[a], inner_im / norms[a]))
        if k:
            re, im = out[k, 0], out[k, 1]
            for a, (r_re, r_im) in enumerate(ratios):
                re = re - (r_re * out[a, 0] - r_im * out[a, 1])
                im = im - (r_re * out[a, 1] + r_im * out[a, 0])
            out[k, 0] = re
            out[k, 1] = im
        norms.append(total(out[k, 0] * out[k, 0] + out[k, 1] * out[k, 1]) + EPSILON)


def gradients(offsets, extended, probe_modes, measured):
    modes, _, size, _ = probe_modes.shape
    layers = extended.shape[0]
    vmem = pl.BlockSpec(memory_space=pltpu.VMEM)
    f32 = jnp.float32
    tables = jnp.asarray(split_tables(size))
    return pl.pallas_call(
        gradient_kernel,
        out_shape=(
            jax.ShapeDtypeStruct(extended.shape, f32),
            jax.ShapeDtypeStruct(probe_modes.shape, f32),
        ),
        in_specs=[pl.BlockSpec(memory_space=pltpu.SMEM), vmem, vmem, vmem, vmem],
        out_specs=(vmem, vmem),
        scratch_shapes=[
            pltpu.VMEM((layers, 2, size, size), f32),
            pltpu.VMEM((max(layers - 1, 1), modes, 2, size, size), f32),
            pltpu.VMEM((modes, 2, size, size), f32),
            pltpu.VMEM((size, size), f32),
            pltpu.VMEM((layers, 2, size, size), f32),
        ],
        compiler_params=pltpu.CompilerParams(vmem_limit_bytes=48 << 20),
    )(offsets, extended, probe_modes, measured, tables)


def halves(top, bottom, lane):
    return jnp.where(lane < HALO, top, bottom)


def exchange_kernel(nx, nc, ext, pgrad, summed, row_bands, col_bands, packed, buf_core, acc_core,
                    buf_x, acc_x, buf_col, send, recv, fold_send, fold_recv):
    modes, _, size, _ = pgrad.shape
    layers, wide = ext.shape[0], ext.shape[3]
    row, col = lax.axis_index("row"), lax.axis_index("col")
    core, x = lax.rem(row, 2), row // 2
    mate = row + 1 - 2 * core
    other = row - 1 + 2 * core
    rows_total = 2 * nx
    has_other = (other >= 0) & (other < rows_total)
    x_peers = [lax.rem(x + d, nx) for d in range(1, nx)]
    col_peers = [lax.rem(col + d, nc) for d in range(1, nc)]
    kind = pl.DeviceIdType.MESH

    barrier = pltpu.get_barrier_semaphore()
    targets = [{"row": mate}]
    targets += [{"row": 2 * peer + core} for peer in x_peers]
    targets += [{"col": peer} for peer in col_peers]
    for target in targets:
        pl.semaphore_signal(barrier, inc=1, device_id=target, device_id_type=kind)

    @pl.when(has_other)
    def _():
        pl.semaphore_signal(barrier, inc=1, device_id={"row": other}, device_id_type=kind)
        pl.semaphore_wait(barrier, len(targets) + 1)

    @pl.when(jnp.logical_not(has_other))
    def _():
        pl.semaphore_wait(barrier, len(targets))

    def remote(src, dst, sems, target):
        return pltpu.make_async_remote_copy(
            src_ref=src, dst_ref=dst, send_sem=sems[0], recv_sem=sems[1],
            device_id=target, device_id_type=kind,
        )

    def sems(m, stage, d):
        return send.at[m, stage, d], recv.at[m, stage, d]

    n = size // nx
    h = 2 * n // nc

    def piece(k):
        return pl.ds(pl.multiple_of((k // 2) * h, h), h), pl.ds(
            pl.multiple_of(lax.rem(k, 2) * 128, 128), 128
        )

    def strip(k):
        return pl.ds(pl.multiple_of(k * n, n), n)

    my_rows, my_lanes = piece(col)
    own_rows = pl.ds(pl.multiple_of(x * n + (col // 2) * h, h), h)

    def stage(m, s):
        if s == 0:
            return [remote(pgrad.at[m, 1 - core], buf_core.at[m], sems(m, s, 0), {"row": mate})]
        if s == 1:
            return [
                remote(acc_core.at[m, strip(peer)], buf_x.at[m, d], sems(m, s, d),
                       {"row": 2 * peer + core})
                for d, peer in enumerate(x_peers)
            ]
        if s == 2:
            return [
                remote(acc_x.at[m, piece(peer)[0], piece(peer)[1]], buf_col.at[m, d],
                       sems(m, s, d), {"col": peer})
                for d, peer in enumerate(col_peers)
            ]
        if s == 3:
            ref = summed.at[m, core, own_rows, my_lanes]
            return [remote(ref, ref, sems(m, s, d), {"col": peer})
                    for d, peer in enumerate(col_peers)]
        if s == 4:
            ref = summed.at[m, core, strip(x)]
            return [remote(ref, ref, sems(m, s, d), {"row": 2 * peer + core})
                    for d, peer in enumerate(x_peers)]
        ref = summed.at[m, core]
        return [remote(ref, ref, sems(m, s, 0), {"row": mate})]

    def finish(m, s):
        for copy in copies[m, s]:
            copy.wait_recv()
        if s == 0:
            acc_core[m] = pgrad[m, core] + buf_core[m]
        if s == 1:
            value = acc_core[m, strip(x)]
            for d in range(nx - 1):
                value = value + buf_x[m, d]
            acc_x[m] = value
        if s == 2:
            value = acc_x[m, my_rows, my_lanes]
            for d in range(nc - 1):
                value = value + buf_col[m, d]
            summed[m, core, own_rows, my_lanes] = value

    copies = {}

    def begin(m, s):
        copies[m, s] = stage(m, s)
        for copy in copies[m, s]:
            copy.start()

    def band(k, axis, at, limit, src, dst):
        inside = (at >= 0) & (at < limit)
        copy = remote(src, dst, (fold_send.at[k], fold_recv.at[k]), {axis: at})
        return inside, copy

    to_high = band(0, "row", row + 1, rows_total,
                   ext.at[:, :, pl.ds(wide - HALO, HALO), :], row_bands.at[0])
    to_low = band(1, "row", row - 1, rows_total, ext.at[:, :, pl.ds(0, HALO), :], row_bands.at[1])
    right = band(2, "col", col + 1, nc, packed.at[0], col_bands.at[0])
    left = band(3, "col", col - 1, nc, packed.at[1], col_bands.at[1])

    def start(pair):
        pl.when(pair[0])(pair[1].start)

    def arrive(pair, inside, ref):
        pl.when(inside)(pair[1].wait_recv)

        @pl.when(jnp.logical_not(inside))
        def _():
            ref[...] = jnp.zeros_like(ref)

    for m in range(modes):
        begin(m, 0)
    start(to_high)
    start(to_low)
    for m in range(modes):
        finish(m, 0)
        begin(m, 1)
    arrive(to_high, row > 0, row_bands.at[0])
    arrive(to_low, row < rows_total - 1, row_bands.at[1])
    lane = lax.broadcasted_iota(jnp.int32, (size // 2, 128), 1)
    for l in range(layers):
        for c in range(2):
            for slot, at in ((0, wide - 128), (1, 0)):
                cut = pl.ds(at, 128)
                half = size // 2
                top = jnp.concatenate([
                    ext[l, c, pl.ds(HALO, HALO), cut] + row_bands[0, l, c, :, cut],
                    ext[l, c, pl.ds(2 * HALO, half - HALO), cut],
                ], axis=0)
                bottom = jnp.concatenate([
                    ext[l, c, pl.ds(HALO + half, half - HALO), cut],
                    ext[l, c, pl.ds(size, HALO), cut] + row_bands[1, l, c, :, cut],
                ], axis=0)
                if slot == 0:
                    top = pltpu.roll(top, HALO, 1)
                else:
                    bottom = pltpu.roll(bottom, HALO, 1)
                packed[slot, l, c] = halves(top, bottom, lane)
    start(right)
    start(left)
    for wave in range(modes + 4):
        for m in range(modes):
            s = 1 + wave - m
            if 1 <= s <= 4:
                finish(m, s)
                begin(m, s + 1)
    for m in range(modes):
        finish(m, 5)
    arrive(right, col > 0, col_bands.at[0])
    arrive(left, col < nc - 1, col_bands.at[1])
    for group in copies.values():
        for copy in group:
            copy.wait_send()
    for pair in (to_high, to_low, right, left):
        pl.when(pair[0])(pair[1].wait_send)


def exchange(grad_ext, local_grad):
    modes, _, size, _ = local_grad.shape
    layers, wide = grad_ext.shape[0], grad_ext.shape[3]
    nx, nc = lax.axis_size("row") // 2, lax.axis_size("col")
    n = size // nx
    h = 2 * n // nc
    f32 = jnp.float32
    vmem = pl.BlockSpec(memory_space=pltpu.VMEM)
    most = max(nx, nc) - 1
    dma = pltpu.SemaphoreType.DMA
    return pl.pallas_call(
        functools.partial(exchange_kernel, nx, nc),
        out_shape=(
            jax.ShapeDtypeStruct(local_grad.shape, f32),
            jax.ShapeDtypeStruct((2, layers, 2, HALO, wide), f32),
            jax.ShapeDtypeStruct((2, layers, 2, size // 2, 128), f32),
        ),
        in_specs=[vmem, vmem],
        out_specs=(vmem, vmem, vmem),
        scratch_shapes=[
            pltpu.VMEM((2, layers, 2, size // 2, 128), f32),
            pltpu.VMEM((modes, size, size), f32),
            pltpu.VMEM((modes, size, size), f32),
            pltpu.VMEM((modes, nx - 1, n, size), f32),
            pltpu.VMEM((modes, n, size), f32),
            pltpu.VMEM((modes, nc - 1, h, 128), f32),
            dma((modes, 6, most)),
            dma((modes, 6, most)),
            dma((4,)),
            dma((4,)),
        ],
        compiler_params=pltpu.CompilerParams(
            collective_id=0, has_side_effects=True, vmem_limit_bytes=48 << 20
        ),
    )(grad_ext, local_grad)


def last_kernel(ext, row_bands, col_bands, probe, summed, grad, out):
    layers, wide = ext.shape[0], ext.shape[3]
    size = grad.shape[3]
    half = size // 2
    lane = lax.broadcasted_iota(jnp.int32, (half, 128), 1)
    for l in range(layers):
        for c in range(2):
            full = jnp.concatenate([
                ext[l, c, pl.ds(HALO, HALO), :] + row_bands[0, l, c],
                ext[l, c, pl.ds(2 * HALO, size - 2 * HALO), :],
                ext[l, c, pl.ds(size, HALO), :] + row_bands[1, l, c],
            ], axis=0)
            full = pltpu.roll(full, wide - HALO, 1)[:, :size]
            low, high = col_bands[0, l, c], col_bands[1, l, c]
            low_turned, high_turned = pltpu.roll(low, HALO, 1), pltpu.roll(high, HALO, 1)
            for at, low_part, high_part in ((0, low, high_turned), (half, low_turned, high)):
                rows = full[at:at + half]
                grad[l, c, pl.ds(at, half), pl.ds(0, 128)] = rows[:, :128] + halves(
                    low_part, 0.0, lane)
                grad[l, c, pl.ds(at, half), pl.ds(size - 128, 128)] = rows[:, 128:] + halves(
                    0.0, high_part, lane)
    update_modes(probe, summed, out)


def last(grad_ext, row_bands, col_bands, probe_modes, summed, grad_shape):
    f32 = jnp.float32
    return pl.pallas_call(
        last_kernel,
        out_shape=(
            jax.ShapeDtypeStruct(grad_shape, f32),
            jax.ShapeDtypeStruct(probe_modes.shape, f32),
        ),
        compiler_params=pltpu.CompilerParams(vmem_limit_bytes=40 << 20),
    )(grad_ext, row_bands, col_bands, probe_modes, summed)


def shards(object_field, probe_modes, measured, offsets):
    extended = with_halo(object_field, (("row", 2), ("col", 3)), HALO)
    grad_ext, local_grad = gradients(offsets, extended, probe_modes, measured)
    summed, row_bands, col_bands = exchange(grad_ext, local_grad)
    return last(grad_ext, row_bands, col_bands, probe_modes, summed, object_field.shape)


def solution(mesh):
    placed = (
        P("grp", None, "row", "col"),
        P("grp", None, None, None),
        P(("grp", "row"), "col", None, None, None),
        P(("grp", "row"), "col", None, None),
    )
    return jax.shard_map(
        shards,
        mesh=mesh,
        in_specs=placed,
        out_specs=(P("grp", None, "row", "col"), P("grp", None, None, None)),
        check_vma=False,
    )
```

```python
import functools
import math

import jax
import jax.numpy as jnp
import numpy as np
from jax import lax
from jax.experimental import pallas as pl
from jax.experimental.pallas import tpu as pltpu
from jax.sharding import PartitionSpec as P

HALO = 64
EPSILON = 1e-06
PROP_PHASE = 40.0


def split_tables(size):
    index = np.arange(size)
    turn = (index[:, None] * index[None, :]) % size
    dft = np.exp(-2j * np.pi * turn / size) / math.sqrt(size)
    freq = ((index + size // 2) % size - size // 2) / size
    prop = np.conj(dft) @ (np.exp(-1j * PROP_PHASE * freq**2)[:, None] * dft)
    stacked = []
    for matrix in (dft, prop):
        for part in (matrix.real, matrix.imag - matrix.real, matrix.imag + matrix.real):
            high = part.astype(jnp.bfloat16)
            low = (part - high.astype(np.float64)).astype(jnp.bfloat16)
            stacked.append(np.stack([high, low]))
    return np.stack(stacked)


def split(value):
    high = value.astype(jnp.bfloat16)
    return high, (value - high.astype(jnp.float32)).astype(jnp.bfloat16)


def mul_right(value, tab, k):
    high, low = split(value)
    t_high, t_low = tab[k, 0], tab[k, 1]
    return jnp.dot(
        jnp.concatenate([high, low, high], axis=1),
        jnp.concatenate([t_high, t_high, t_low], axis=0),
        preferred_element_type=jnp.float32,
    )


def mul_left(value, tab, k):
    high, low = split(value)
    t_high, t_low = tab[k, 0], tab[k, 1]
    return jnp.dot(
        jnp.concatenate([t_high, t_high, t_low], axis=1),
        jnp.concatenate([high, low, high], axis=0),
        preferred_element_type=jnp.float32,
    )


def both_sides(re, im, tab, base, conj):
    for mul in (mul_right, mul_left):
        both = mul(re + im, tab, base)
        if conj:
            re, im = both + mul(im, tab, base + 1), both - mul(re, tab, base + 2)
        else:
            re, im = both - mul(im, tab, base + 2), both + mul(re, tab, base + 1)
    return re, im


def gradient_kernel(offs, ext, probe, meas, tab, grad, pgrad, win, wave, far, inten, terms):
    modes, size = probe.shape[0], probe.shape[2]
    layers, wide = ext.shape[0], ext.shape[3]
    positions = meas.shape[2]
    grad[...] = jnp.zeros_like(grad)
    pgrad[...] = jnp.zeros_like(pgrad)

    def position(p, carry):
        row = offs[0, 0, p, 0] + HALO
        col = offs[0, 0, p, 1] + HALO
        base = pl.multiple_of(jnp.minimum(row // 8, (2 * HALO - 8) // 8) * 8, 8)
        rest = row - base
        tall = size + 8
        for l in range(layers):
            for c in range(2):
                rows = ext[l, c, pl.ds(base, tall), :]
                rows = pltpu.roll(rows, lax.rem(wide - col, wide), 1)[:, :size]
                win[l, c] = pltpu.roll(rows, lax.rem(tall - rest, tall), 0)[:size]
        inten[...] = -meas[0, 0, p]
        terms[...] = jnp.zeros_like(terms)
        last = layers - 1

        def forward(m, carry):
            re, im = probe[m, 0], probe[m, 1]
            for l in range(layers):
                t_re, t_im = win[l, 0], win[l, 1]
                e_re = t_re * re - t_im * im
                e_im = t_re * im + t_im * re
                if l < last:
                    re, im = both_sides(e_re, e_im, tab, 3, False)
                    wave[l, m, 0] = re
                    wave[l, m, 1] = im
                else:
                    re, im = both_sides(e_re, e_im, tab, 0, False)
            far[m, 0] = re
            far[m, 1] = im
            inten[...] += re * re + im * im
            return carry

        lax.fori_loop(0, modes, forward, 0, unroll=UNROLL)

        def backward(m, carry):
            misfit = inten[...]
            re, im = both_sides(misfit * far[m, 0], misfit * far[m, 1], tab, 0, True)
            for l in range(last, -1, -1):
                w_re = wave[l - 1, m, 0] if l > 0 else probe[m, 0]
                w_im = wave[l - 1, m, 1] if l > 0 else probe[m, 1]
                terms[l, 0] += w_re * re + w_im * im
                terms[l, 1] += w_re * im - w_im * re
                t_re, t_im = win[l, 0], win[l, 1]
                b_re = t_re * re + t_im * im
                b_im = t_re * im - t_im * re
                if l > 0:
                    re, im = both_sides(b_re, b_im, tab, 3, True)
                else:
                    pgrad[m, 0] += b_re
                    pgrad[m, 1] += b_im
            return carry

        lax.fori_loop(0, modes, backward, 0, unroll=UNROLL)
        for l in range(layers):
            for c in range(2):
                padded = jnp.concatenate([terms[l, c], jnp.zeros((8, size), jnp.float32)], axis=0)
                padded = pltpu.roll(padded, rest, 0)
                padded = jnp.concatenate(
                    [padded, jnp.zeros((tall, wide - size), jnp.float32)], axis=1
                )
                grad[l, c, pl.ds(base, tall), :] += pltpu.roll(padded, col, 1)
        return carry

    lax.fori_loop(0, positions, position, 0)


UNROLL = True


def total(value):
    return jnp.sum(jnp.sum(value, axis=0, keepdims=True), axis=1, keepdims=True)


def update_modes(probe, summed, out):
    modes = probe.shape[0]
    probe_sq = total(sum(probe[m, c] * probe[m, c] for m in range(modes) for c in range(2)))
    grad_sq = total(sum(summed[m, c] * summed[m, c] for m in range(modes) for c in range(2)))
    factor = 0.5 * jnp.sqrt(probe_sq / (grad_sq + EPSILON))
    norms = []
    for k in range(modes):
        out[k, 0] = probe[k, 0] - factor * summed[k, 0]
        out[k, 1] = probe[k, 1] - factor * summed[k, 1]
        ratios = []
        for a in range(k):
            inner_re = total(out[a, 0] * out[k, 0] + out[a, 1] * out[k, 1])
            inner_im = total(out[a, 0] * out[k, 1] - out[a, 1] * out[k, 0])
            ratios.append((inner_re / norms[a], inner_im / norms[a]))
        if k:
            re, im = out[k, 0], out[k, 1]
            for a, (r_re, r_im) in enumerate(ratios):
                re = re - (r_re * out[a, 0] - r_im * out[a, 1])
                im = im - (r_re * out[a, 1] + r_im * out[a, 0])
            out[k, 0] = re
            out[k, 1] = im
        norms.append(total(out[k, 0] * out[k, 0] + out[k, 1] * out[k, 1]) + EPSILON)


def gradients(offsets, extended, probe_modes, measured):
    modes, _, size, _ = probe_modes.shape
    layers = extended.shape[0]
    vmem = pl.BlockSpec(memory_space=pltpu.VMEM)
    f32 = jnp.float32
    tables = jnp.asarray(split_tables(size))
    return pl.pallas_call(
        gradient_kernel,
        out_shape=(
            jax.ShapeDtypeStruct(extended.shape, f32),
            jax.ShapeDtypeStruct(probe_modes.shape, f32),
        ),
        in_specs=[pl.BlockSpec(memory_space=pltpu.SMEM), vmem, vmem, vmem, vmem],
        out_specs=(vmem, vmem),
        scratch_shapes=[
            pltpu.VMEM((layers, 2, size, size), f32),
            pltpu.VMEM((max(layers - 1, 1), modes, 2, size, size), f32),
            pltpu.VMEM((modes, 2, size, size), f32),
            pltpu.VMEM((size, size), f32),
            pltpu.VMEM((layers, 2, size, size), f32),
        ],
        compiler_params=pltpu.CompilerParams(vmem_limit_bytes=48 << 20),
    )(offsets, extended, probe_modes, measured, tables)


def halves(top, bottom, lane):
    return jnp.where(lane < HALO, top, bottom)


def halo_kernel(nr, nc, field, ext, packed, row_bands, corners, col_bands, col_corners, send, recv):
    layers, _, size, _ = field.shape
    half = size // 2
    row, col = lax.axis_index("row"), lax.axis_index("col")
    kind = pl.DeviceIdType.MESH
    barrier = pltpu.get_barrier_semaphore()
    for target in (
        {"row": lax.rem(row + 1, nr)},
        {"row": lax.rem(row + nr - 1, nr)},
        {"col": lax.rem(col + 1, nc)},
        {"col": lax.rem(col + nc - 1, nc)},
    ):
        pl.semaphore_signal(barrier, inc=1, device_id=target, device_id_type=kind)

    planes = [(l, c) for l in range(layers) for c in range(2)]
    lane = lax.broadcasted_iota(jnp.int32, (half, 128), 1)
    edge = lax.broadcasted_iota(jnp.int32, (HALO, 128), 1)
    for l, c in planes:
        top, bottom = field[l, c, pl.ds(0, half)], field[l, c, pl.ds(half, half)]
        packed[0, l, c] = halves(pltpu.roll(top[:, size - 128:], HALO, 1), bottom[:, size - 128:],
                                 lane)
        packed[1, l, c] = halves(top[:, :128], pltpu.roll(bottom[:, :128], HALO, 1), lane)
    pl.semaphore_wait(barrier, 4)

    def route(k, axis, at, limit, src, dst):
        copy = pltpu.make_async_remote_copy(
            src_ref=src, dst_ref=dst, send_sem=send.at[k], recv_sem=recv.at[k],
            device_id={axis: at}, device_id_type=kind,
        )
        return (at >= 0) & (at < limit), copy

    def start(pair):
        pl.when(pair[0])(pair[1].start)

    def arrive(pair, inside, ref):
        pl.when(inside)(pair[1].wait_recv)

        @pl.when(jnp.logical_not(inside))
        def _():
            ref[...] = jnp.zeros_like(ref)

    to_high = route(0, "row", row + 1, nr, field.at[:, :, pl.ds(size - HALO, HALO)],
                    row_bands.at[0])
    to_low = route(1, "row", row - 1, nr, field.at[:, :, pl.ds(0, HALO)], row_bands.at[1])
    right = route(2, "col", col + 1, nc, packed.at[0], col_bands.at[0])
    left = route(3, "col", col - 1, nc, packed.at[1], col_bands.at[1])
    right_corner = route(4, "col", col + 1, nc, corners.at[0], col_corners.at[0])
    left_corner = route(5, "col", col - 1, nc, corners.at[1], col_corners.at[1])
    start(to_high)
    start(to_low)
    start(right)
    start(left)
    arrive(to_high, row > 0, row_bands.at[0])
    arrive(to_low, row < nr - 1, row_bands.at[1])
    for l, c in planes:
        low, high = row_bands[0, l, c], row_bands[1, l, c]
        corners[0, l, c] = halves(pltpu.roll(low[:, size - 128:], HALO, 1), high[:, size - 128:],
                                  edge)
        corners[1, l, c] = halves(low[:, :128], pltpu.roll(high[:, :128], HALO, 1), edge)
    start(right_corner)
    start(left_corner)

    def middle(l, c):
        at = 0
        for part in (row_bands[0, l, c], field[l, c], row_bands[1, l, c]):
            tall = part.shape[0]
            turned = [pltpu.roll(part[:, k:k + 128], HALO, 1) for k in range(0, size, 128)]
            mask = lax.broadcasted_iota(jnp.int32, (tall, 128), 1)
            spot = pl.ds(at, tall)
            for k in range(len(turned) + 1):
                before = turned[k - 1] if k else 0.0
                after = turned[k] if k < len(turned) else 0.0
                ext[l, c, spot, pl.ds(128 * k, 128)] = halves(before, after, mask)
            at += tall

    for l, c in planes:
        middle(l, c)
    wide = ext.shape[3]
    first, final = pl.ds(0, 128), pl.ds(wide - 128, 128)

    def sides(low_side, high_side, l, c, at, tall, mask):
        low, high = low_side[l, c], high_side[l, c]
        low_turned, high_turned = pltpu.roll(low, HALO, 1), pltpu.roll(high, HALO, 1)
        for spot, low_part, high_part in (
            (pl.ds(at[0], tall), low, high_turned),
            (pl.ds(at[1], tall), low_turned, high),
        ):
            ext[l, c, spot, first] = halves(low_part, ext[l, c, spot, first], mask)
            ext[l, c, spot, final] = halves(ext[l, c, spot, final], high_part, mask)

    arrive(right, col > 0, col_bands.at[0])
    arrive(left, col < nc - 1, col_bands.at[1])
    for l, c in planes:
        sides(col_bands.at[0], col_bands.at[1], l, c, (HALO, HALO + half), half, lane)
    arrive(right_corner, col > 0, col_corners.at[0])
    arrive(left_corner, col < nc - 1, col_corners.at[1])
    for l, c in planes:
        sides(col_corners.at[0], col_corners.at[1], l, c, (0, HALO + size), HALO, edge)
    for pair in (to_high, to_low, right, left, right_corner, left_corner):
        pl.when(pair[0])(pair[1].wait_send)


def with_halo(field):
    layers, _, size, _ = field.shape
    wide = size + 2 * HALO
    f32 = jnp.float32
    vmem = pl.BlockSpec(memory_space=pltpu.VMEM)
    dma = pltpu.SemaphoreType.DMA
    side = pltpu.VMEM((2, layers, 2, size // 2, 128), f32)
    corner = pltpu.VMEM((2, layers, 2, HALO, 128), f32)
    return pl.pallas_call(
        functools.partial(halo_kernel, lax.axis_size("row"), lax.axis_size("col")),
        out_shape=jax.ShapeDtypeStruct((layers, 2, wide, wide), f32),
        in_specs=[vmem],
        out_specs=vmem,
        scratch_shapes=[
            side,
            pltpu.VMEM((2, layers, 2, HALO, size), f32),
            corner,
            side,
            corner,
            dma((6,)),
            dma((6,)),
        ],
        compiler_params=pltpu.CompilerParams(
            collective_id=1, has_side_effects=True, vmem_limit_bytes=32 << 20
        ),
    )(field)


def exchange_kernel(nx, nc, ext, pgrad, summed, row_bands, col_bands, packed, buf_core, acc_core,
                    buf_x, acc_x, buf_col, send, recv, fold_send, fold_recv):
    modes, _, size, _ = pgrad.shape
    layers, wide = ext.shape[0], ext.shape[3]
    row, col = lax.axis_index("row"), lax.axis_index("col")
    core, x = lax.rem(row, 2), row // 2
    mate = row + 1 - 2 * core
    other = row - 1 + 2 * core
    rows_total = 2 * nx
    has_other = (other >= 0) & (other < rows_total)
    x_peers = [lax.rem(x + d, nx) for d in range(1, nx)]
    col_peers = [lax.rem(col + d, nc) for d in range(1, nc)]
    kind = pl.DeviceIdType.MESH

    barrier = pltpu.get_barrier_semaphore()
    targets = [{"row": mate}]
    targets += [{"row": 2 * peer + core} for peer in x_peers]
    targets += [{"col": peer} for peer in col_peers]
    for target in targets:
        pl.semaphore_signal(barrier, inc=1, device_id=target, device_id_type=kind)

    @pl.when(has_other)
    def _():
        pl.semaphore_signal(barrier, inc=1, device_id={"row": other}, device_id_type=kind)
        pl.semaphore_wait(barrier, len(targets) + 1)

    @pl.when(jnp.logical_not(has_other))
    def _():
        pl.semaphore_wait(barrier, len(targets))

    def remote(src, dst, sems, target):
        return pltpu.make_async_remote_copy(
            src_ref=src, dst_ref=dst, send_sem=sems[0], recv_sem=sems[1],
            device_id=target, device_id_type=kind,
        )

    def sems(m, stage, d):
        return send.at[m, stage, d], recv.at[m, stage, d]

    n = size // nx
    h = 2 * n // nc

    def piece(k):
        return pl.ds(pl.multiple_of((k // 2) * h, h), h), pl.ds(
            pl.multiple_of(lax.rem(k, 2) * 128, 128), 128
        )

    def strip(k):
        return pl.ds(pl.multiple_of(k * n, n), n)

    my_rows, my_lanes = piece(col)
    own_rows = pl.ds(pl.multiple_of(x * n + (col // 2) * h, h), h)

    def stage(m, s):
        if s == 0:
            return [remote(pgrad.at[m, 1 - core], buf_core.at[m], sems(m, s, 0), {"row": mate})]
        if s == 1:
            return [
                remote(acc_core.at[m, strip(peer)], buf_x.at[m, d], sems(m, s, d),
                       {"row": 2 * peer + core})
                for d, peer in enumerate(x_peers)
            ]
        if s == 2:
            return [
                remote(acc_x.at[m, piece(peer)[0], piece(peer)[1]], buf_col.at[m, d],
                       sems(m, s, d), {"col": peer})
                for d, peer in enumerate(col_peers)
            ]
        if s == 3:
            ref = summed.at[m, core, own_rows, my_lanes]
            return [remote(ref, ref, sems(m, s, d), {"col": peer})
                    for d, peer in enumerate(col_peers)]
        if s == 4:
            ref = summed.at[m, core, strip(x)]
            return [remote(ref, ref, sems(m, s, d), {"row": 2 * peer + core})
                    for d, peer in enumerate(x_peers)]
        ref = summed.at[m, core]
        return [remote(ref, ref, sems(m, s, 0), {"row": mate})]

    def finish(m, s):
        for copy in copies[m, s]:
            copy.wait_recv()
        if s == 0:
            acc_core[m] = pgrad[m, core] + buf_core[m]
        if s == 1:
            value = acc_core[m, strip(x)]
            for d in range(nx - 1):
                value = value + buf_x[m, d]
            acc_x[m] = value
        if s == 2:
            value = acc_x[m, my_rows, my_lanes]
            for d in range(nc - 1):
                value = value + buf_col[m, d]
            summed[m, core, own_rows, my_lanes] = value

    copies = {}

    def begin(m, s):
        copies[m, s] = stage(m, s)
        for copy in copies[m, s]:
            copy.start()

    def band(k, axis, at, limit, src, dst):
        inside = (at >= 0) & (at < limit)
        copy = remote(src, dst, (fold_send.at[k], fold_recv.at[k]), {axis: at})
        return inside, copy

    to_high = band(0, "row", row + 1, rows_total,
                   ext.at[:, :, pl.ds(wide - HALO, HALO), :], row_bands.at[0])
    to_low = band(1, "row", row - 1, rows_total, ext.at[:, :, pl.ds(0, HALO), :], row_bands.at[1])
    right = band(2, "col", col + 1, nc, packed.at[0], col_bands.at[0])
    left = band(3, "col", col - 1, nc, packed.at[1], col_bands.at[1])

    def start(pair):
        pl.when(pair[0])(pair[1].start)

    def arrive(pair, inside, ref):
        pl.when(inside)(pair[1].wait_recv)

        @pl.when(jnp.logical_not(inside))
        def _():
            ref[...] = jnp.zeros_like(ref)

    for m in range(modes):
        begin(m, 0)
    start(to_high)
    start(to_low)
    for m in range(modes):
        finish(m, 0)
        begin(m, 1)
    arrive(to_high, row > 0, row_bands.at[0])
    arrive(to_low, row < rows_total - 1, row_bands.at[1])
    lane = lax.broadcasted_iota(jnp.int32, (size // 2, 128), 1)
    for l in range(layers):
        for c in range(2):
            for slot, at in ((0, wide - 128), (1, 0)):
                cut = pl.ds(at, 128)
                half = size // 2
                top = jnp.concatenate([
                    ext[l, c, pl.ds(HALO, HALO), cut] + row_bands[0, l, c, :, cut],
                    ext[l, c, pl.ds(2 * HALO, half - HALO), cut],
                ], axis=0)
                bottom = jnp.concatenate([
                    ext[l, c, pl.ds(HALO + half, half - HALO), cut],
                    ext[l, c, pl.ds(size, HALO), cut] + row_bands[1, l, c, :, cut],
                ], axis=0)
                if slot == 0:
                    top = pltpu.roll(top, HALO, 1)
                else:
                    bottom = pltpu.roll(bottom, HALO, 1)
                packed[slot, l, c] = halves(top, bottom, lane)
    start(right)
    start(left)
    for wave in range(modes + 4):
        for m in range(modes):
            s = 1 + wave - m
            if 1 <= s <= 4:
                finish(m, s)
                begin(m, s + 1)
    for m in range(modes):
        finish(m, 5)
    arrive(right, col > 0, col_bands.at[0])
    arrive(left, col < nc - 1, col_bands.at[1])
    for group in copies.values():
        for copy in group:
            copy.wait_send()
    for pair in (to_high, to_low, right, left):
        pl.when(pair[0])(pair[1].wait_send)


def exchange(grad_ext, local_grad):
    modes, _, size, _ = local_grad.shape
    layers, wide = grad_ext.shape[0], grad_ext.shape[3]
    nx, nc = lax.axis_size("row") // 2, lax.axis_size("col")
    n = size // nx
    h = 2 * n // nc
    f32 = jnp.float32
    vmem = pl.BlockSpec(memory_space=pltpu.VMEM)
    most = max(nx, nc) - 1
    dma = pltpu.SemaphoreType.DMA
    return pl.pallas_call(
        functools.partial(exchange_kernel, nx, nc),
        out_shape=(
            jax.ShapeDtypeStruct(local_grad.shape, f32),
            jax.ShapeDtypeStruct((2, layers, 2, HALO, wide), f32),
            jax.ShapeDtypeStruct((2, layers, 2, size // 2, 128), f32),
        ),
        in_specs=[vmem, vmem],
        out_specs=(vmem, vmem, vmem),
        scratch_shapes=[
            pltpu.VMEM((2, layers, 2, size // 2, 128), f32),
            pltpu.VMEM((modes, size, size), f32),
            pltpu.VMEM((modes, size, size), f32),
            pltpu.VMEM((modes, nx - 1, n, size), f32),
            pltpu.VMEM((modes, n, size), f32),
            pltpu.VMEM((modes, nc - 1, h, 128), f32),
            dma((modes, 6, most)),
            dma((modes, 6, most)),
            dma((4,)),
            dma((4,)),
        ],
        compiler_params=pltpu.CompilerParams(
            collective_id=0, has_side_effects=True, vmem_limit_bytes=48 << 20
        ),
    )(grad_ext, local_grad)


def last_kernel(ext, row_bands, col_bands, probe, summed, grad, out):
    layers, wide = ext.shape[0], ext.shape[3]
    size = grad.shape[3]
    half = size // 2
    lane = lax.broadcasted_iota(jnp.int32, (half, 128), 1)
    for l in range(layers):
        for c in range(2):
            full = jnp.concatenate([
                ext[l, c, pl.ds(HALO, HALO), :] + row_bands[0, l, c],
                ext[l, c, pl.ds(2 * HALO, size - 2 * HALO), :],
                ext[l, c, pl.ds(size, HALO), :] + row_bands[1, l, c],
            ], axis=0)
            full = pltpu.roll(full, wide - HALO, 1)[:, :size]
            low, high = col_bands[0, l, c], col_bands[1, l, c]
            low_turned, high_turned = pltpu.roll(low, HALO, 1), pltpu.roll(high, HALO, 1)
            for at, low_part, high_part in ((0, low, high_turned), (half, low_turned, high)):
                rows = full[at:at + half]
                grad[l, c, pl.ds(at, half), pl.ds(0, 128)] = rows[:, :128] + halves(
                    low_part, 0.0, lane)
                grad[l, c, pl.ds(at, half), pl.ds(size - 128, 128)] = rows[:, 128:] + halves(
                    0.0, high_part, lane)
    update_modes(probe, summed, out)


def last(grad_ext, row_bands, col_bands, probe_modes, summed, grad_shape):
    f32 = jnp.float32
    return pl.pallas_call(
        last_kernel,
        out_shape=(
            jax.ShapeDtypeStruct(grad_shape, f32),
            jax.ShapeDtypeStruct(probe_modes.shape, f32),
        ),
        compiler_params=pltpu.CompilerParams(vmem_limit_bytes=40 << 20),
    )(grad_ext, row_bands, col_bands, probe_modes, summed)


def shards(object_field, probe_modes, measured, offsets):
    extended = with_halo(object_field)
    grad_ext, local_grad = gradients(offsets, extended, probe_modes, measured)
    summed, row_bands, col_bands = exchange(grad_ext, local_grad)
    return last(grad_ext, row_bands, col_bands, probe_modes, summed, object_field.shape)


def solution(mesh):
    placed = (
        P("grp", None, "row", "col"),
        P("grp", None, None, None),
        P(("grp", "row"), "col", None, None, None),
        P(("grp", "row"), "col", None, None),
    )
    return jax.shard_map(
        shards,
        mesh=mesh,
        in_specs=placed,
        out_specs=(P("grp", None, "row", "col"), P("grp", None, None, None)),
        check_vma=False,
    )
```

```python
import functools
import math

import jax
import jax.numpy as jnp
import numpy as np
from jax import lax
from jax.experimental import pallas as pl
from jax.experimental.pallas import tpu as pltpu
from jax.sharding import PartitionSpec as P

HALO = 64
EPSILON = 1e-06
PROP_PHASE = 40.0


def split_tables(size):
    index = np.arange(size)
    turn = (index[:, None] * index[None, :]) % size
    dft = np.exp(-2j * np.pi * turn / size) / math.sqrt(size)
    freq = ((index + size // 2) % size - size // 2) / size
    prop = np.conj(dft) @ (np.exp(-1j * PROP_PHASE * freq**2)[:, None] * dft)
    stacked = []
    for matrix in (dft, prop):
        for part in (matrix.real, matrix.imag - matrix.real, matrix.imag + matrix.real):
            high = part.astype(jnp.bfloat16)
            low = (part - high.astype(np.float64)).astype(jnp.bfloat16)
            stacked.append(np.stack([high, low]))
    return np.stack(stacked)


def split(value):
    high = value.astype(jnp.bfloat16)
    return high, (value - high.astype(jnp.float32)).astype(jnp.bfloat16)


def mul_right(value, tab, k):
    high, low = split(value)
    t_high, t_low = tab[k, 0], tab[k, 1]
    return jnp.dot(
        jnp.concatenate([high, low, high], axis=1),
        jnp.concatenate([t_high, t_high, t_low], axis=0),
        preferred_element_type=jnp.float32,
    )


def mul_left(value, tab, k):
    high, low = split(value)
    t_high, t_low = tab[k, 0], tab[k, 1]
    return jnp.dot(
        jnp.concatenate([t_high, t_high, t_low], axis=1),
        jnp.concatenate([high, low, high], axis=0),
        preferred_element_type=jnp.float32,
    )


def both_sides(re, im, tab, base, conj):
    for mul in (mul_right, mul_left):
        both = mul(re + im, tab, base)
        if conj:
            re, im = both + mul(im, tab, base + 1), both - mul(re, tab, base + 2)
        else:
            re, im = both - mul(im, tab, base + 2), both + mul(re, tab, base + 1)
    return re, im


def gradient_kernel(offs, ext, probe, meas, tab, grad, pgrad, win, wave, far, inten, terms):
    modes, size = probe.shape[0], probe.shape[2]
    layers, wide = ext.shape[0], ext.shape[3]
    positions = meas.shape[2]
    grad[...] = jnp.zeros_like(grad)
    pgrad[...] = jnp.zeros_like(pgrad)

    def position(p, carry):
        row = offs[0, 0, p, 0] + HALO
        col = offs[0, 0, p, 1] + HALO
        base = pl.multiple_of(jnp.minimum(row // 8, (2 * HALO - 8) // 8) * 8, 8)
        rest = row - base
        tall = size + 8
        for l in range(layers):
            for c in range(2):
                rows = ext[l, c, pl.ds(base, tall), :]
                rows = pltpu.roll(rows, lax.rem(wide - col, wide), 1)[:, :size]
                win[l, c] = pltpu.roll(rows, lax.rem(tall - rest, tall), 0)[:size]
        inten[...] = -meas[0, 0, p]
        terms[...] = jnp.zeros_like(terms)
        last = layers - 1

        def forward(m, carry):
            re, im = probe[m, 0], probe[m, 1]
            for l in range(layers):
                t_re, t_im = win[l, 0], win[l, 1]
                e_re = t_re * re - t_im * im
                e_im = t_re * im + t_im * re
                if l < last:
                    re, im = both_sides(e_re, e_im, tab, 3, False)
                    wave[l, m, 0] = re
                    wave[l, m, 1] = im
                else:
                    re, im = both_sides(e_re, e_im, tab, 0, False)
            far[m, 0] = re
            far[m, 1] = im
            inten[...] += re * re + im * im
            return carry

        lax.fori_loop(0, modes, forward, 0, unroll=UNROLL)

        def backward(m, carry):
            misfit = inten[...]
            re, im = both_sides(misfit * far[m, 0], misfit * far[m, 1], tab, 0, True)
            for l in range(last, -1, -1):
                w_re = wave[l - 1, m, 0] if l > 0 else probe[m, 0]
                w_im = wave[l - 1, m, 1] if l > 0 else probe[m, 1]
                terms[l, 0] += w_re * re + w_im * im
                terms[l, 1] += w_re * im - w_im * re
                t_re, t_im = win[l, 0], win[l, 1]
                b_re = t_re * re + t_im * im
                b_im = t_re * im - t_im * re
                if l > 0:
                    re, im = both_sides(b_re, b_im, tab, 3, True)
                else:
                    pgrad[m, 0] += b_re
                    pgrad[m, 1] += b_im
            return carry

        lax.fori_loop(0, modes, backward, 0, unroll=UNROLL)
        for l in range(layers):
            for c in range(2):
                padded = jnp.concatenate([terms[l, c], jnp.zeros((8, size), jnp.float32)], axis=0)
                padded = pltpu.roll(padded, rest, 0)
                padded = jnp.concatenate(
                    [padded, jnp.zeros((tall, wide - size), jnp.float32)], axis=1
                )
                grad[l, c, pl.ds(base, tall), :] += pltpu.roll(padded, col, 1)
        return carry

    lax.fori_loop(0, positions, position, 0)


UNROLL = True


def total(value):
    return jnp.sum(jnp.sum(value, axis=0, keepdims=True), axis=1, keepdims=True)


def update_modes(probe, summed, out):
    modes = probe.shape[0]
    probe_sq = total(sum(probe[m, c] * probe[m, c] for m in range(modes) for c in range(2)))
    grad_sq = total(sum(summed[m, c] * summed[m, c] for m in range(modes) for c in range(2)))
    factor = 0.5 * jnp.sqrt(probe_sq / (grad_sq + EPSILON))
    norms = []
    for k in range(modes):
        out[k, 0] = probe[k, 0] - factor * summed[k, 0]
        out[k, 1] = probe[k, 1] - factor * summed[k, 1]
        ratios = []
        for a in range(k):
            inner_re = total(out[a, 0] * out[k, 0] + out[a, 1] * out[k, 1])
            inner_im = total(out[a, 0] * out[k, 1] - out[a, 1] * out[k, 0])
            ratios.append((inner_re / norms[a], inner_im / norms[a]))
        if k:
            re, im = out[k, 0], out[k, 1]
            for a, (r_re, r_im) in enumerate(ratios):
                re = re - (r_re * out[a, 0] - r_im * out[a, 1])
                im = im - (r_re * out[a, 1] + r_im * out[a, 0])
            out[k, 0] = re
            out[k, 1] = im
        norms.append(total(out[k, 0] * out[k, 0] + out[k, 1] * out[k, 1]) + EPSILON)


def gradients(offsets, extended, probe_modes, measured):
    modes, _, size, _ = probe_modes.shape
    layers = extended.shape[0]
    vmem = pl.BlockSpec(memory_space=pltpu.VMEM)
    f32 = jnp.float32
    tables = jnp.asarray(split_tables(size))
    return pl.pallas_call(
        gradient_kernel,
        out_shape=(
            jax.ShapeDtypeStruct(extended.shape, f32),
            jax.ShapeDtypeStruct(probe_modes.shape, f32),
        ),
        in_specs=[pl.BlockSpec(memory_space=pltpu.SMEM), vmem, vmem, vmem, vmem],
        out_specs=(vmem, vmem),
        scratch_shapes=[
            pltpu.VMEM((layers, 2, size, size), f32),
            pltpu.VMEM((max(layers - 1, 1), modes, 2, size, size), f32),
            pltpu.VMEM((modes, 2, size, size), f32),
            pltpu.VMEM((size, size), f32),
            pltpu.VMEM((layers, 2, size, size), f32),
        ],
        compiler_params=pltpu.CompilerParams(vmem_limit_bytes=48 << 20),
    )(offsets, extended, probe_modes, measured, tables)


def halves(top, bottom, lane):
    return jnp.where(lane < HALO, top, bottom)


def halo_kernel(nr, nc, field, ext, packed, row_bands, corners, col_bands, col_corners, send, recv):
    layers, _, size, _ = field.shape
    half = size // 2
    row, col = lax.axis_index("row"), lax.axis_index("col")
    kind = pl.DeviceIdType.MESH
    barrier = pltpu.get_barrier_semaphore()
    for target in (
        {"row": lax.rem(row + 1, nr)},
        {"row": lax.rem(row + nr - 1, nr)},
        {"col": lax.rem(col + 1, nc)},
        {"col": lax.rem(col + nc - 1, nc)},
    ):
        pl.semaphore_signal(barrier, inc=1, device_id=target, device_id_type=kind)

    planes = [(l, c) for l in range(layers) for c in range(2)]
    lane = lax.broadcasted_iota(jnp.int32, (half, 128), 1)
    edge = lax.broadcasted_iota(jnp.int32, (HALO, 128), 1)
    for l, c in planes:
        top, bottom = field[l, c, pl.ds(0, half)], field[l, c, pl.ds(half, half)]
        packed[0, l, c] = halves(pltpu.roll(top[:, size - 128:], HALO, 1), bottom[:, size - 128:],
                                 lane)
        packed[1, l, c] = halves(top[:, :128], pltpu.roll(bottom[:, :128], HALO, 1), lane)
    pl.semaphore_wait(barrier, 4)

    def route(k, axis, at, limit, src, dst):
        copy = pltpu.make_async_remote_copy(
            src_ref=src, dst_ref=dst, send_sem=send.at[k], recv_sem=recv.at[k],
            device_id={axis: at}, device_id_type=kind,
        )
        return (at >= 0) & (at < limit), copy

    def start(pair):
        pl.when(pair[0])(pair[1].start)

    def arrive(pair, inside, ref):
        pl.when(inside)(pair[1].wait_recv)

        @pl.when(jnp.logical_not(inside))
        def _():
            ref[...] = jnp.zeros_like(ref)

    to_high = route(0, "row", row + 1, nr, field.at[:, :, pl.ds(size - HALO, HALO)],
                    row_bands.at[0])
    to_low = route(1, "row", row - 1, nr, field.at[:, :, pl.ds(0, HALO)], row_bands.at[1])
    right = route(2, "col", col + 1, nc, packed.at[0], col_bands.at[0])
    left = route(3, "col", col - 1, nc, packed.at[1], col_bands.at[1])
    right_corner = route(4, "col", col + 1, nc, corners.at[0], col_corners.at[0])
    left_corner = route(5, "col", col - 1, nc, corners.at[1], col_corners.at[1])
    start(to_high)
    start(to_low)
    start(right)
    start(left)
    arrive(to_high, row > 0, row_bands.at[0])
    arrive(to_low, row < nr - 1, row_bands.at[1])
    for l, c in planes:
        low, high = row_bands[0, l, c], row_bands[1, l, c]
        corners[0, l, c] = halves(pltpu.roll(low[:, size - 128:], HALO, 1), high[:, size - 128:],
                                  edge)
        corners[1, l, c] = halves(low[:, :128], pltpu.roll(high[:, :128], HALO, 1), edge)
    start(right_corner)
    start(left_corner)

    def middle(l, c):
        at = 0
        for part in (row_bands[0, l, c], field[l, c], row_bands[1, l, c]):
            tall = part.shape[0]
            turned = [pltpu.roll(part[:, k:k + 128], HALO, 1) for k in range(0, size, 128)]
            mask = lax.broadcasted_iota(jnp.int32, (tall, 128), 1)
            spot = pl.ds(at, tall)
            for k in range(len(turned) + 1):
                before = turned[k - 1] if k else 0.0
                after = turned[k] if k < len(turned) else 0.0
                ext[l, c, spot, pl.ds(128 * k, 128)] = halves(before, after, mask)
            at += tall

    for l, c in planes:
        middle(l, c)
    wide = ext.shape[3]
    first, final = pl.ds(0, 128), pl.ds(wide - 128, 128)

    def sides(low_side, high_side, l, c, at, tall, mask):
        low, high = low_side[l, c], high_side[l, c]
        low_turned, high_turned = pltpu.roll(low, HALO, 1), pltpu.roll(high, HALO, 1)
        for spot, low_part, high_part in (
            (pl.ds(at[0], tall), low, high_turned),
            (pl.ds(at[1], tall), low_turned, high),
        ):
            ext[l, c, spot, first] = halves(low_part, ext[l, c, spot, first], mask)
            ext[l, c, spot, final] = halves(ext[l, c, spot, final], high_part, mask)

    arrive(right, col > 0, col_bands.at[0])
    arrive(left, col < nc - 1, col_bands.at[1])
    for l, c in planes:
        sides(col_bands.at[0], col_bands.at[1], l, c, (HALO, HALO + half), half, lane)
    arrive(right_corner, col > 0, col_corners.at[0])
    arrive(left_corner, col < nc - 1, col_corners.at[1])
    for l, c in planes:
        sides(col_corners.at[0], col_corners.at[1], l, c, (0, HALO + size), HALO, edge)
    for pair in (to_high, to_low, right, left, right_corner, left_corner):
        pl.when(pair[0])(pair[1].wait_send)


def with_halo(field):
    layers, _, size, _ = field.shape
    wide = size + 2 * HALO
    f32 = jnp.float32
    vmem = pl.BlockSpec(memory_space=pltpu.VMEM)
    dma = pltpu.SemaphoreType.DMA
    side = pltpu.VMEM((2, layers, 2, size // 2, 128), f32)
    corner = pltpu.VMEM((2, layers, 2, HALO, 128), f32)
    return pl.pallas_call(
        functools.partial(halo_kernel, lax.axis_size("row"), lax.axis_size("col")),
        out_shape=jax.ShapeDtypeStruct((layers, 2, wide, wide), f32),
        in_specs=[vmem],
        out_specs=vmem,
        scratch_shapes=[
            side,
            pltpu.VMEM((2, layers, 2, HALO, size), f32),
            corner,
            side,
            corner,
            dma((6,)),
            dma((6,)),
        ],
        compiler_params=pltpu.CompilerParams(
            collective_id=1, has_side_effects=True, vmem_limit_bytes=32 << 20
        ),
    )(field)


def exchange_kernel(nx, nc, ext, pgrad, summed, row_bands, col_bands, packed, buf_core, acc_core,
                    buf_x, acc_x, buf_col, send, recv, fold_send, fold_recv):
    modes, _, size, _ = pgrad.shape
    layers, wide = ext.shape[0], ext.shape[3]
    row, col = lax.axis_index("row"), lax.axis_index("col")
    core, x = lax.rem(row, 2), row // 2
    mate = row + 1 - 2 * core
    other = row - 1 + 2 * core
    rows_total = 2 * nx
    has_other = (other >= 0) & (other < rows_total)
    x_peers = [lax.rem(x + d, nx) for d in range(1, nx)]
    col_peers = [lax.rem(col + d, nc) for d in range(1, nc)]
    kind = pl.DeviceIdType.MESH

    barrier = pltpu.get_barrier_semaphore()
    targets = [{"row": mate}]
    targets += [{"row": 2 * peer + core} for peer in x_peers]
    targets += [{"col": peer} for peer in col_peers]
    for target in targets:
        pl.semaphore_signal(barrier, inc=1, device_id=target, device_id_type=kind)

    @pl.when(has_other)
    def _():
        pl.semaphore_signal(barrier, inc=1, device_id={"row": other}, device_id_type=kind)
        pl.semaphore_wait(barrier, len(targets) + 1)

    @pl.when(jnp.logical_not(has_other))
    def _():
        pl.semaphore_wait(barrier, len(targets))

    def remote(src, dst, sems, target):
        return pltpu.make_async_remote_copy(
            src_ref=src, dst_ref=dst, send_sem=sems[0], recv_sem=sems[1],
            device_id=target, device_id_type=kind,
        )

    def sems(m, stage, d):
        return send.at[m, stage, d], recv.at[m, stage, d]

    n = size // nx
    h = 2 * n // nc

    def piece(k):
        return pl.ds(pl.multiple_of((k // 2) * h, h), h), pl.ds(
            pl.multiple_of(lax.rem(k, 2) * 128, 128), 128
        )

    def strip(k):
        return pl.ds(pl.multiple_of(k * n, n), n)

    my_rows, my_lanes = piece(col)
    own_rows = pl.ds(pl.multiple_of(x * n + (col // 2) * h, h), h)

    def stage(m, s):
        if s == 0:
            return [remote(pgrad.at[m, 1 - core], buf_core.at[m], sems(m, s, 0), {"row": mate})]
        if s == 1:
            return [
                remote(acc_core.at[m, strip(peer)], buf_x.at[m, d], sems(m, s, d),
                       {"row": 2 * peer + core})
                for d, peer in enumerate(x_peers)
            ]
        if s == 2:
            return [
                remote(acc_x.at[m, piece(peer)[0], piece(peer)[1]], buf_col.at[m, d],
                       sems(m, s, d), {"col": peer})
                for d, peer in enumerate(col_peers)
            ]
        if s == 3:
            ref = summed.at[m, core, own_rows, my_lanes]
            return [remote(ref, ref, sems(m, s, d), {"col": peer})
                    for d, peer in enumerate(col_peers)]
        if s == 4:
            ref = summed.at[m, core, strip(x)]
            return [remote(ref, ref, sems(m, s, d), {"row": 2 * peer + core})
                    for d, peer in enumerate(x_peers)]
        ref = summed.at[m, core]
        return [remote(ref, ref, sems(m, s, 0), {"row": mate})]

    def finish(m, s):
        for copy in copies[m, s]:
            copy.wait_recv()
        if s == 0:
            acc_core[m] = pgrad[m, core] + buf_core[m]
        if s == 1:
            value = acc_core[m, strip(x)]
            for d in range(nx - 1):
                value = value + buf_x[m, d]
            acc_x[m] = value
        if s == 2:
            value = acc_x[m, my_rows, my_lanes]
            for d in range(nc - 1):
                value = value + buf_col[m, d]
            summed[m, core, own_rows, my_lanes] = value

    copies = {}

    def begin(m, s):
        copies[m, s] = stage(m, s)
        for copy in copies[m, s]:
            copy.start()

    def band(k, axis, at, limit, src, dst):
        inside = (at >= 0) & (at < limit)
        copy = remote(src, dst, (fold_send.at[k], fold_recv.at[k]), {axis: at})
        return inside, copy

    to_high = band(0, "row", row + 1, rows_total,
                   ext.at[:, :, pl.ds(wide - HALO, HALO), :], row_bands.at[0])
    to_low = band(1, "row", row - 1, rows_total, ext.at[:, :, pl.ds(0, HALO), :], row_bands.at[1])
    right = band(2, "col", col + 1, nc, packed.at[0], col_bands.at[0])
    left = band(3, "col", col - 1, nc, packed.at[1], col_bands.at[1])

    def start(pair):
        pl.when(pair[0])(pair[1].start)

    def arrive(pair, inside, ref):
        pl.when(inside)(pair[1].wait_recv)

        @pl.when(jnp.logical_not(inside))
        def _():
            ref[...] = jnp.zeros_like(ref)

    for m in range(modes):
        begin(m, 0)
    for m in range(modes):
        finish(m, 0)
        begin(m, 1)
    start(to_high)
    start(to_low)

    def pack():
        arrive(to_high, row > 0, row_bands.at[0])
        arrive(to_low, row < rows_total - 1, row_bands.at[1])
        lane = lax.broadcasted_iota(jnp.int32, (size // 2, 128), 1)
        for l in range(layers):
            for c in range(2):
                for slot, at in ((0, wide - 128), (1, 0)):
                    cut = pl.ds(at, 128)
                    half = size // 2
                    top = jnp.concatenate([
                        ext[l, c, pl.ds(HALO, HALO), cut] + row_bands[0, l, c, :, cut],
                        ext[l, c, pl.ds(2 * HALO, half - HALO), cut],
                    ], axis=0)
                    bottom = jnp.concatenate([
                        ext[l, c, pl.ds(HALO + half, half - HALO), cut],
                        ext[l, c, pl.ds(size, HALO), cut] + row_bands[1, l, c, :, cut],
                    ], axis=0)
                    if slot == 0:
                        top = pltpu.roll(top, HALO, 1)
                    else:
                        bottom = pltpu.roll(bottom, HALO, 1)
                    packed[slot, l, c] = halves(top, bottom, lane)

    for wave in range(modes + 3):
        for m in range(modes):
            s = 1 + wave - m
            if 1 <= s <= 4:
                finish(m, s)
                begin(m, s + 1)
        if wave == modes - 1:
            pack()
        if wave == modes:
            start(right)
            start(left)
    for m in range(modes):
        finish(m, 5)
    arrive(right, col > 0, col_bands.at[0])
    arrive(left, col < nc - 1, col_bands.at[1])
    for group in copies.values():
        for copy in group:
            copy.wait_send()
    for pair in (to_high, to_low, right, left):
        pl.when(pair[0])(pair[1].wait_send)


def exchange(grad_ext, local_grad):
    modes, _, size, _ = local_grad.shape
    layers, wide = grad_ext.shape[0], grad_ext.shape[3]
    nx, nc = lax.axis_size("row") // 2, lax.axis_size("col")
    n = size // nx
    h = 2 * n // nc
    f32 = jnp.float32
    vmem = pl.BlockSpec(memory_space=pltpu.VMEM)
    most = max(nx, nc) - 1
    dma = pltpu.SemaphoreType.DMA
    return pl.pallas_call(
        functools.partial(exchange_kernel, nx, nc),
        out_shape=(
            jax.ShapeDtypeStruct(local_grad.shape, f32),
            jax.ShapeDtypeStruct((2, layers, 2, HALO, wide), f32),
            jax.ShapeDtypeStruct((2, layers, 2, size // 2, 128), f32),
        ),
        in_specs=[vmem, vmem],
        out_specs=(vmem, vmem, vmem),
        scratch_shapes=[
            pltpu.VMEM((2, layers, 2, size // 2, 128), f32),
            pltpu.VMEM((modes, size, size), f32),
            pltpu.VMEM((modes, size, size), f32),
            pltpu.VMEM((modes, nx - 1, n, size), f32),
            pltpu.VMEM((modes, n, size), f32),
            pltpu.VMEM((modes, nc - 1, h, 128), f32),
            dma((modes, 6, most)),
            dma((modes, 6, most)),
            dma((4,)),
            dma((4,)),
        ],
        compiler_params=pltpu.CompilerParams(
            collective_id=0, has_side_effects=True, vmem_limit_bytes=48 << 20
        ),
    )(grad_ext, local_grad)


def last_kernel(ext, row_bands, col_bands, probe, summed, grad, out):
    layers, wide = ext.shape[0], ext.shape[3]
    size = grad.shape[3]
    half = size // 2
    lane = lax.broadcasted_iota(jnp.int32, (half, 128), 1)
    for l in range(layers):
        for c in range(2):
            full = jnp.concatenate([
                ext[l, c, pl.ds(HALO, HALO), :] + row_bands[0, l, c],
                ext[l, c, pl.ds(2 * HALO, size - 2 * HALO), :],
                ext[l, c, pl.ds(size, HALO), :] + row_bands[1, l, c],
            ], axis=0)
            full = pltpu.roll(full, wide - HALO, 1)[:, :size]
            low, high = col_bands[0, l, c], col_bands[1, l, c]
            low_turned, high_turned = pltpu.roll(low, HALO, 1), pltpu.roll(high, HALO, 1)
            for at, low_part, high_part in ((0, low, high_turned), (half, low_turned, high)):
                rows = full[at:at + half]
                grad[l, c, pl.ds(at, half), pl.ds(0, 128)] = rows[:, :128] + halves(
                    low_part, 0.0, lane)
                grad[l, c, pl.ds(at, half), pl.ds(size - 128, 128)] = rows[:, 128:] + halves(
                    0.0, high_part, lane)
    update_modes(probe, summed, out)


def last(grad_ext, row_bands, col_bands, probe_modes, summed, grad_shape):
    f32 = jnp.float32
    return pl.pallas_call(
        last_kernel,
        out_shape=(
            jax.ShapeDtypeStruct(grad_shape, f32),
            jax.ShapeDtypeStruct(probe_modes.shape, f32),
        ),
        compiler_params=pltpu.CompilerParams(vmem_limit_bytes=40 << 20),
    )(grad_ext, row_bands, col_bands, probe_modes, summed)


def shards(object_field, probe_modes, measured, offsets):
    extended = with_halo(object_field)
    grad_ext, local_grad = gradients(offsets, extended, probe_modes, measured)
    summed, row_bands, col_bands = exchange(grad_ext, local_grad)
    return last(grad_ext, row_bands, col_bands, probe_modes, summed, object_field.shape)


def solution(mesh):
    placed = (
        P("grp", None, "row", "col"),
        P("grp", None, None, None),
        P(("grp", "row"), "col", None, None, None),
        P(("grp", "row"), "col", None, None),
    )
    return jax.shard_map(
        shards,
        mesh=mesh,
        in_specs=placed,
        out_specs=(P("grp", None, "row", "col"), P("grp", None, None, None)),
        check_vma=False,
    )
```

```python
import functools
import math

import jax
import jax.numpy as jnp
import numpy as np
from jax import lax
from jax.experimental import pallas as pl
from jax.experimental.pallas import tpu as pltpu
from jax.sharding import PartitionSpec as P

HALO = 64
EPSILON = 1e-06
PROP_PHASE = 40.0


def split_tables(size):
    index = np.arange(size)
    turn = (index[:, None] * index[None, :]) % size
    dft = np.exp(-2j * np.pi * turn / size) / math.sqrt(size)
    freq = ((index + size // 2) % size - size // 2) / size
    prop = np.conj(dft) @ (np.exp(-1j * PROP_PHASE * freq**2)[:, None] * dft)
    stacked = []
    for matrix in (dft, prop):
        for part in (matrix.real, matrix.imag - matrix.real, matrix.imag + matrix.real):
            high = part.astype(jnp.bfloat16)
            low = (part - high.astype(np.float64)).astype(jnp.bfloat16)
            stacked.append(np.stack([high, low]))
    return np.stack(stacked)


def split(value):
    high = value.astype(jnp.bfloat16)
    return high, (value - high.astype(jnp.float32)).astype(jnp.bfloat16)


def mul_right(value, tab, k):
    high, low = split(value)
    t_high, t_low = tab[k, 0], tab[k, 1]
    return jnp.dot(
        jnp.concatenate([high, low, high], axis=1),
        jnp.concatenate([t_high, t_high, t_low], axis=0),
        preferred_element_type=jnp.float32,
    )


def mul_left(value, tab, k):
    high, low = split(value)
    t_high, t_low = tab[k, 0], tab[k, 1]
    return jnp.dot(
        jnp.concatenate([t_high, t_high, t_low], axis=1),
        jnp.concatenate([high, low, high], axis=0),
        preferred_element_type=jnp.float32,
    )


def both_sides(re, im, tab, base, conj):
    for mul in (mul_right, mul_left):
        both = mul(re + im, tab, base)
        if conj:
            re, im = both + mul(im, tab, base + 1), both - mul(re, tab, base + 2)
        else:
            re, im = both - mul(im, tab, base + 2), both + mul(re, tab, base + 1)
    return re, im


def gradient_kernel(offs, ext, probe, meas, tab, grad, pgrad, win, wave, far, inten, terms):
    modes, size = probe.shape[0], probe.shape[2]
    layers, wide = ext.shape[0], ext.shape[3]
    positions = meas.shape[2]
    grad[...] = jnp.zeros_like(grad)
    pgrad[...] = jnp.zeros_like(pgrad)

    def position(p, carry):
        row = offs[0, 0, p, 0] + HALO
        col = offs[0, 0, p, 1] + HALO
        base = pl.multiple_of(jnp.minimum(row // 8, (2 * HALO - 8) // 8) * 8, 8)
        rest = row - base
        tall = size + 8
        for l in range(layers):
            for c in range(2):
                rows = ext[l, c, pl.ds(base, tall), :]
                rows = pltpu.roll(rows, lax.rem(wide - col, wide), 1)[:, :size]
                win[l, c] = pltpu.roll(rows, lax.rem(tall - rest, tall), 0)[:size]
        inten[...] = -meas[0, 0, p]
        terms[...] = jnp.zeros_like(terms)
        last = layers - 1

        def forward(m, carry):
            re, im = probe[m, 0], probe[m, 1]
            for l in range(layers):
                t_re, t_im = win[l, 0], win[l, 1]
                e_re = t_re * re - t_im * im
                e_im = t_re * im + t_im * re
                if l < last:
                    re, im = both_sides(e_re, e_im, tab, 3, False)
                    wave[l, m, 0] = re
                    wave[l, m, 1] = im
                else:
                    re, im = both_sides(e_re, e_im, tab, 0, False)
            far[m, 0] = re
            far[m, 1] = im
            inten[...] += re * re + im * im
            return carry

        lax.fori_loop(0, modes, forward, 0, unroll=UNROLL)

        def backward(m, carry):
            misfit = inten[...]
            re, im = both_sides(misfit * far[m, 0], misfit * far[m, 1], tab, 0, True)
            for l in range(last, -1, -1):
                w_re = wave[l - 1, m, 0] if l > 0 else probe[m, 0]
                w_im = wave[l - 1, m, 1] if l > 0 else probe[m, 1]
                terms[l, 0] += w_re * re + w_im * im
                terms[l, 1] += w_re * im - w_im * re
                t_re, t_im = win[l, 0], win[l, 1]
                b_re = t_re * re + t_im * im
                b_im = t_re * im - t_im * re
                if l > 0:
                    re, im = both_sides(b_re, b_im, tab, 3, True)
                else:
                    pgrad[m, 0] += b_re
                    pgrad[m, 1] += b_im
            return carry

        lax.fori_loop(0, modes, backward, 0, unroll=UNROLL)
        for l in range(layers):
            for c in range(2):
                padded = jnp.concatenate([terms[l, c], jnp.zeros((8, size), jnp.float32)], axis=0)
                padded = pltpu.roll(padded, rest, 0)
                padded = jnp.concatenate(
                    [padded, jnp.zeros((tall, wide - size), jnp.float32)], axis=1
                )
                grad[l, c, pl.ds(base, tall), :] += pltpu.roll(padded, col, 1)
        return carry

    lax.fori_loop(0, positions, position, 0)


UNROLL = True


def total(value):
    return jnp.sum(jnp.sum(value, axis=0, keepdims=True), axis=1, keepdims=True)


def update_modes(probe, summed, out):
    modes = probe.shape[0]
    probe_sq = total(sum(probe[m, c] * probe[m, c] for m in range(modes) for c in range(2)))
    grad_sq = total(sum(summed[m, c] * summed[m, c] for m in range(modes) for c in range(2)))
    factor = 0.5 * jnp.sqrt(probe_sq / (grad_sq + EPSILON))
    norms = []
    for k in range(modes):
        out[k, 0] = probe[k, 0] - factor * summed[k, 0]
        out[k, 1] = probe[k, 1] - factor * summed[k, 1]
        ratios = []
        for a in range(k):
            inner_re = total(out[a, 0] * out[k, 0] + out[a, 1] * out[k, 1])
            inner_im = total(out[a, 0] * out[k, 1] - out[a, 1] * out[k, 0])
            ratios.append((inner_re / norms[a], inner_im / norms[a]))
        if k:
            re, im = out[k, 0], out[k, 1]
            for a, (r_re, r_im) in enumerate(ratios):
                re = re - (r_re * out[a, 0] - r_im * out[a, 1])
                im = im - (r_re * out[a, 1] + r_im * out[a, 0])
            out[k, 0] = re
            out[k, 1] = im
        norms.append(total(out[k, 0] * out[k, 0] + out[k, 1] * out[k, 1]) + EPSILON)


def gradients(offsets, extended, probe_modes, measured):
    modes, _, size, _ = probe_modes.shape
    layers = extended.shape[0]
    vmem = pl.BlockSpec(memory_space=pltpu.VMEM)
    f32 = jnp.float32
    tables = jnp.asarray(split_tables(size))
    return pl.pallas_call(
        gradient_kernel,
        out_shape=(
            jax.ShapeDtypeStruct(extended.shape, f32),
            jax.ShapeDtypeStruct(probe_modes.shape, f32),
        ),
        in_specs=[pl.BlockSpec(memory_space=pltpu.SMEM), vmem, vmem, vmem, vmem],
        out_specs=(vmem, vmem),
        scratch_shapes=[
            pltpu.VMEM((layers, 2, size, size), f32),
            pltpu.VMEM((max(layers - 1, 1), modes, 2, size, size), f32),
            pltpu.VMEM((modes, 2, size, size), f32),
            pltpu.VMEM((size, size), f32),
            pltpu.VMEM((layers, 2, size, size), f32),
        ],
        compiler_params=pltpu.CompilerParams(vmem_limit_bytes=28 << 20),
    )(offsets, extended, probe_modes, measured, tables)


def halves(top, bottom, lane):
    return jnp.where(lane < HALO, top, bottom)


def halo_kernel(nr, nc, field, ext, packed, row_bands, corners, col_bands, col_corners, send, recv):
    layers, _, size, _ = field.shape
    half = size // 2
    row, col = lax.axis_index("row"), lax.axis_index("col")
    kind = pl.DeviceIdType.MESH
    barrier = pltpu.get_barrier_semaphore()
    for target in (
        {"row": lax.rem(row + 1, nr)},
        {"row": lax.rem(row + nr - 1, nr)},
        {"col": lax.rem(col + 1, nc)},
        {"col": lax.rem(col + nc - 1, nc)},
    ):
        pl.semaphore_signal(barrier, inc=1, device_id=target, device_id_type=kind)

    planes = [(l, c) for l in range(layers) for c in range(2)]
    lane = lax.broadcasted_iota(jnp.int32, (half, 128), 1)
    edge = lax.broadcasted_iota(jnp.int32, (HALO, 128), 1)
    for l, c in planes:
        top, bottom = field[l, c, pl.ds(0, half)], field[l, c, pl.ds(half, half)]
        packed[0, l, c] = halves(pltpu.roll(top[:, size - 128:], HALO, 1), bottom[:, size - 128:],
                                 lane)
        packed[1, l, c] = halves(top[:, :128], pltpu.roll(bottom[:, :128], HALO, 1), lane)
    pl.semaphore_wait(barrier, 4)

    def route(k, axis, at, limit, src, dst):
        copy = pltpu.make_async_remote_copy(
            src_ref=src, dst_ref=dst, send_sem=send.at[k], recv_sem=recv.at[k],
            device_id={axis: at}, device_id_type=kind,
        )
        return (at >= 0) & (at < limit), copy

    def start(pair):
        pl.when(pair[0])(pair[1].start)

    def arrive(pair, inside, ref):
        pl.when(inside)(pair[1].wait_recv)

        @pl.when(jnp.logical_not(inside))
        def _():
            ref[...] = jnp.zeros_like(ref)

    to_high = route(0, "row", row + 1, nr, field.at[:, :, pl.ds(size - HALO, HALO)],
                    row_bands.at[0])
    to_low = route(1, "row", row - 1, nr, field.at[:, :, pl.ds(0, HALO)], row_bands.at[1])
    right = route(2, "col", col + 1, nc, packed.at[0], col_bands.at[0])
    left = route(3, "col", col - 1, nc, packed.at[1], col_bands.at[1])
    right_corner = route(4, "col", col + 1, nc, corners.at[0], col_corners.at[0])
    left_corner = route(5, "col", col - 1, nc, corners.at[1], col_corners.at[1])
    start(to_high)
    start(to_low)
    start(right)
    start(left)
    arrive(to_high, row > 0, row_bands.at[0])
    arrive(to_low, row < nr - 1, row_bands.at[1])
    for l, c in planes:
        low, high = row_bands[0, l, c], row_bands[1, l, c]
        corners[0, l, c] = halves(pltpu.roll(low[:, size - 128:], HALO, 1), high[:, size - 128:],
                                  edge)
        corners[1, l, c] = halves(low[:, :128], pltpu.roll(high[:, :128], HALO, 1), edge)
    start(right_corner)
    start(left_corner)

    def middle(l, c):
        at = 0
        for part in (row_bands[0, l, c], field[l, c], row_bands[1, l, c]):
            tall = part.shape[0]
            turned = [pltpu.roll(part[:, k:k + 128], HALO, 1) for k in range(0, size, 128)]
            mask = lax.broadcasted_iota(jnp.int32, (tall, 128), 1)
            spot = pl.ds(at, tall)
            for k in range(len(turned) + 1):
                before = turned[k - 1] if k else 0.0
                after = turned[k] if k < len(turned) else 0.0
                ext[l, c, spot, pl.ds(128 * k, 128)] = halves(before, after, mask)
            at += tall

    for l, c in planes:
        middle(l, c)
    wide = ext.shape[3]
    first, final = pl.ds(0, 128), pl.ds(wide - 128, 128)

    def sides(low_side, high_side, l, c, at, tall, mask):
        low, high = low_side[l, c], high_side[l, c]
        low_turned, high_turned = pltpu.roll(low, HALO, 1), pltpu.roll(high, HALO, 1)
        for spot, low_part, high_part in (
            (pl.ds(at[0], tall), low, high_turned),
            (pl.ds(at[1], tall), low_turned, high),
        ):
            ext[l, c, spot, first] = halves(low_part, ext[l, c, spot, first], mask)
            ext[l, c, spot, final] = halves(ext[l, c, spot, final], high_part, mask)

    arrive(right, col > 0, col_bands.at[0])
    arrive(left, col < nc - 1, col_bands.at[1])
    for l, c in planes:
        sides(col_bands.at[0], col_bands.at[1], l, c, (HALO, HALO + half), half, lane)
    arrive(right_corner, col > 0, col_corners.at[0])
    arrive(left_corner, col < nc - 1, col_corners.at[1])
    for l, c in planes:
        sides(col_corners.at[0], col_corners.at[1], l, c, (0, HALO + size), HALO, edge)
    for pair in (to_high, to_low, right, left, right_corner, left_corner):
        pl.when(pair[0])(pair[1].wait_send)


def with_halo(field):
    layers, _, size, _ = field.shape
    wide = size + 2 * HALO
    f32 = jnp.float32
    vmem = pl.BlockSpec(memory_space=pltpu.VMEM)
    dma = pltpu.SemaphoreType.DMA
    side = pltpu.VMEM((2, layers, 2, size // 2, 128), f32)
    corner = pltpu.VMEM((2, layers, 2, HALO, 128), f32)
    return pl.pallas_call(
        functools.partial(halo_kernel, lax.axis_size("row"), lax.axis_size("col")),
        out_shape=jax.ShapeDtypeStruct((layers, 2, wide, wide), f32),
        in_specs=[vmem],
        out_specs=vmem,
        scratch_shapes=[
            side,
            pltpu.VMEM((2, layers, 2, HALO, size), f32),
            corner,
            side,
            corner,
            dma((6,)),
            dma((6,)),
        ],
        compiler_params=pltpu.CompilerParams(
            collective_id=1, has_side_effects=True, vmem_limit_bytes=20 << 20
        ),
    )(field)


def exchange_kernel(nx, nc, ext, pgrad, summed, row_bands, col_bands, packed, buf_core, acc_core,
                    buf_x, acc_x, buf_col, send, recv, fold_send, fold_recv):
    modes, _, size, _ = pgrad.shape
    layers, wide = ext.shape[0], ext.shape[3]
    row, col = lax.axis_index("row"), lax.axis_index("col")
    core, x = lax.rem(row, 2), row // 2
    mate = row + 1 - 2 * core
    other = row - 1 + 2 * core
    rows_total = 2 * nx
    has_other = (other >= 0) & (other < rows_total)
    x_peers = [lax.rem(x + d, nx) for d in range(1, nx)]
    col_peers = [lax.rem(col + d, nc) for d in range(1, nc)]
    kind = pl.DeviceIdType.MESH

    barrier = pltpu.get_barrier_semaphore()
    targets = [{"row": mate}]
    targets += [{"row": 2 * peer + core} for peer in x_peers]
    targets += [{"col": peer} for peer in col_peers]
    for target in targets:
        pl.semaphore_signal(barrier, inc=1, device_id=target, device_id_type=kind)

    @pl.when(has_other)
    def _():
        pl.semaphore_signal(barrier, inc=1, device_id={"row": other}, device_id_type=kind)
        pl.semaphore_wait(barrier, len(targets) + 1)

    @pl.when(jnp.logical_not(has_other))
    def _():
        pl.semaphore_wait(barrier, len(targets))

    def remote(src, dst, sems, target):
        return pltpu.make_async_remote_copy(
            src_ref=src, dst_ref=dst, send_sem=sems[0], recv_sem=sems[1],
            device_id=target, device_id_type=kind,
        )

    def sems(m, stage, d):
        return send.at[m, stage, d], recv.at[m, stage, d]

    n = size // nx
    h = 2 * n // nc

    def piece(k):
        return pl.ds(pl.multiple_of((k // 2) * h, h), h), pl.ds(
            pl.multiple_of(lax.rem(k, 2) * 128, 128), 128
        )

    def strip(k):
        return pl.ds(pl.multiple_of(k * n, n), n)

    my_rows, my_lanes = piece(col)
    own_rows = pl.ds(pl.multiple_of(x * n + (col // 2) * h, h), h)

    def stage(m, s):
        if s == 0:
            return [remote(pgrad.at[m, 1 - core], buf_core.at[m], sems(m, s, 0), {"row": mate})]
        if s == 1:
            return [
                remote(acc_core.at[m, strip(peer)], buf_x.at[m, d], sems(m, s, d),
                       {"row": 2 * peer + core})
                for d, peer in enumerate(x_peers)
            ]
        if s == 2:
            return [
                remote(acc_x.at[m, piece(peer)[0], piece(peer)[1]], buf_col.at[m, d],
                       sems(m, s, d), {"col": peer})
                for d, peer in enumerate(col_peers)
            ]
        if s == 3:
            ref = summed.at[m, core, own_rows, my_lanes]
            return [remote(ref, ref, sems(m, s, d), {"col": peer})
                    for d, peer in enumerate(col_peers)]
        if s == 4:
            ref = summed.at[m, core, strip(x)]
            return [remote(ref, ref, sems(m, s, d), {"row": 2 * peer + core})
                    for d, peer in enumerate(x_peers)]
        ref = summed.at[m, core]
        return [remote(ref, ref, sems(m, s, 0), {"row": mate})]

    def finish(m, s):
        for copy in copies[m, s]:
            copy.wait_recv()
        if s == 0:
            acc_core[m] = pgrad[m, core] + buf_core[m]
        if s == 1:
            value = acc_core[m, strip(x)]
            for d in range(nx - 1):
                value = value + buf_x[m, d]
            acc_x[m] = value
        if s == 2:
            value = acc_x[m, my_rows, my_lanes]
            for d in range(nc - 1):
                value = value + buf_col[m, d]
            summed[m, core, own_rows, my_lanes] = value

    copies = {}

    def begin(m, s):
        copies[m, s] = stage(m, s)
        for copy in copies[m, s]:
            copy.start()

    def band(k, axis, at, limit, src, dst):
        inside = (at >= 0) & (at < limit)
        copy = remote(src, dst, (fold_send.at[k], fold_recv.at[k]), {axis: at})
        return inside, copy

    to_high = band(0, "row", row + 1, rows_total,
                   ext.at[:, :, pl.ds(wide - HALO, HALO), :], row_bands.at[0])
    to_low = band(1, "row", row - 1, rows_total, ext.at[:, :, pl.ds(0, HALO), :], row_bands.at[1])
    right = band(2, "col", col + 1, nc, packed.at[0], col_bands.at[0])
    left = band(3, "col", col - 1, nc, packed.at[1], col_bands.at[1])

    def start(pair):
        pl.when(pair[0])(pair[1].start)

    def arrive(pair, inside, ref):
        pl.when(inside)(pair[1].wait_recv)

        @pl.when(jnp.logical_not(inside))
        def _():
            ref[...] = jnp.zeros_like(ref)

    for m in range(modes):
        begin(m, 0)
    for m in range(modes):
        finish(m, 0)
        begin(m, 1)
    start(to_high)
    start(to_low)

    def pack():
        arrive(to_high, row > 0, row_bands.at[0])
        arrive(to_low, row < rows_total - 1, row_bands.at[1])
        lane = lax.broadcasted_iota(jnp.int32, (size // 2, 128), 1)
        for l in range(layers):
            for c in range(2):
                for slot, at in ((0, wide - 128), (1, 0)):
                    cut = pl.ds(at, 128)
                    half = size // 2
                    top = jnp.concatenate([
                        ext[l, c, pl.ds(HALO, HALO), cut] + row_bands[0, l, c, :, cut],
                        ext[l, c, pl.ds(2 * HALO, half - HALO), cut],
                    ], axis=0)
                    bottom = jnp.concatenate([
                        ext[l, c, pl.ds(HALO + half, half - HALO), cut],
                        ext[l, c, pl.ds(size, HALO), cut] + row_bands[1, l, c, :, cut],
                    ], axis=0)
                    if slot == 0:
                        top = pltpu.roll(top, HALO, 1)
                    else:
                        bottom = pltpu.roll(bottom, HALO, 1)
                    packed[slot, l, c] = halves(top, bottom, lane)

    for wave in range(modes + 3):
        for m in range(modes):
            s = 1 + wave - m
            if 1 <= s <= 4:
                finish(m, s)
                begin(m, s + 1)
        if wave == modes - 1:
            pack()
        if wave == modes:
            start(right)
            start(left)
    for m in range(modes):
        finish(m, 5)
    arrive(right, col > 0, col_bands.at[0])
    arrive(left, col < nc - 1, col_bands.at[1])
    for group in copies.values():
        for copy in group:
            copy.wait_send()
    for pair in (to_high, to_low, right, left):
        pl.when(pair[0])(pair[1].wait_send)


def exchange(grad_ext, local_grad):
    modes, _, size, _ = local_grad.shape
    layers, wide = grad_ext.shape[0], grad_ext.shape[3]
    nx, nc = lax.axis_size("row") // 2, lax.axis_size("col")
    n = size // nx
    h = 2 * n // nc
    f32 = jnp.float32
    vmem = pl.BlockSpec(memory_space=pltpu.VMEM)
    most = max(nx, nc) - 1
    dma = pltpu.SemaphoreType.DMA
    return pl.pallas_call(
        functools.partial(exchange_kernel, nx, nc),
        out_shape=(
            jax.ShapeDtypeStruct(local_grad.shape, f32),
            jax.ShapeDtypeStruct((2, layers, 2, HALO, wide), f32),
            jax.ShapeDtypeStruct((2, layers, 2, size // 2, 128), f32),
        ),
        in_specs=[vmem, vmem],
        out_specs=(vmem, vmem, vmem),
        scratch_shapes=[
            pltpu.VMEM((2, layers, 2, size // 2, 128), f32),
            pltpu.VMEM((modes, size, size), f32),
            pltpu.VMEM((modes, size, size), f32),
            pltpu.VMEM((modes, nx - 1, n, size), f32),
            pltpu.VMEM((modes, n, size), f32),
            pltpu.VMEM((modes, nc - 1, h, 128), f32),
            dma((modes, 6, most)),
            dma((modes, 6, most)),
            dma((4,)),
            dma((4,)),
        ],
        compiler_params=pltpu.CompilerParams(
            collective_id=0, has_side_effects=True, vmem_limit_bytes=28 << 20
        ),
    )(grad_ext, local_grad)


def last_kernel(ext, row_bands, col_bands, probe, summed, grad, out):
    layers, wide = ext.shape[0], ext.shape[3]
    size = grad.shape[3]
    half = size // 2
    lane = lax.broadcasted_iota(jnp.int32, (half, 128), 1)
    for l in range(layers):
        for c in range(2):
            full = jnp.concatenate([
                ext[l, c, pl.ds(HALO, HALO), :] + row_bands[0, l, c],
                ext[l, c, pl.ds(2 * HALO, size - 2 * HALO), :],
                ext[l, c, pl.ds(size, HALO), :] + row_bands[1, l, c],
            ], axis=0)
            full = pltpu.roll(full, wide - HALO, 1)[:, :size]
            low, high = col_bands[0, l, c], col_bands[1, l, c]
            low_turned, high_turned = pltpu.roll(low, HALO, 1), pltpu.roll(high, HALO, 1)
            for at, low_part, high_part in ((0, low, high_turned), (half, low_turned, high)):
                rows = full[at:at + half]
                grad[l, c, pl.ds(at, half), pl.ds(0, 128)] = rows[:, :128] + halves(
                    low_part, 0.0, lane)
                grad[l, c, pl.ds(at, half), pl.ds(size - 128, 128)] = rows[:, 128:] + halves(
                    0.0, high_part, lane)
    update_modes(probe, summed, out)


def last(grad_ext, row_bands, col_bands, probe_modes, summed, grad_shape):
    f32 = jnp.float32
    return pl.pallas_call(
        last_kernel,
        out_shape=(
            jax.ShapeDtypeStruct(grad_shape, f32),
            jax.ShapeDtypeStruct(probe_modes.shape, f32),
        ),
        compiler_params=pltpu.CompilerParams(vmem_limit_bytes=24 << 20),
    )(grad_ext, row_bands, col_bands, probe_modes, summed)


def shards(object_field, probe_modes, measured, offsets):
    extended = with_halo(object_field)
    grad_ext, local_grad = gradients(offsets, extended, probe_modes, measured)
    summed, row_bands, col_bands = exchange(grad_ext, local_grad)
    return last(grad_ext, row_bands, col_bands, probe_modes, summed, object_field.shape)


def solution(mesh):
    placed = (
        P("grp", None, "row", "col"),
        P("grp", None, None, None),
        P(("grp", "row"), "col", None, None, None),
        P(("grp", "row"), "col", None, None),
    )
    return jax.shard_map(
        shards,
        mesh=mesh,
        in_specs=placed,
        out_specs=(P("grp", None, "row", "col"), P("grp", None, None, None)),
        check_vma=False,
    )
```
